32 devices in a mesh: row: 4 (over y, x), seq: 8 (over z, core).
Axes of the slice: x: 2, y: 2, z: 4, core: 2. Of those that a mesh axis runs over, the one named last changes fastest.
Arguments:
- hidden_in: bfloat16 [4, 1024, 1024], P('row', 'seq'), may hold values from -6 to 6
- segments: int32 [4, 1024], P('row', 'seq'), may hold values from 0 to 2, as said below
- routes: int32 [4, 1024, 8], P('row', 'seq'), may hold values from 0 to 15, all different within a row; in each aligned block of 128 rows (0 to 127, 128 to 255, ..., all dimensions but the last counted through in order) at most 80 rows name the same one
- cotangent: bfloat16 [4, 1024, 1024], P('row', 'seq'), may hold values from -6 to 6
- attn_gain: bfloat16 [1024], P(('row', 'seq')), may hold values from 0.5 to 1.5
- query_weight: bfloat16 [1024, 1024], P(('row', 'seq')), may hold values from -0.1875 to 0.1875
- key_weight: bfloat16 [1024, 512], P(('row', 'seq')), may hold values from -0.1875 to 0.1875
- value_weight: bfloat16 [1024, 512], P(('row', 'seq')), may hold values from -0.1875 to 0.1875
- out_weight: bfloat16 [1024, 1024], P(None, ('row', 'seq')), may hold values from -0.75 to 0.75
- ffn_gain: bfloat16 [1024], P(('row', 'seq')), may hold values from 0.5 to 1.5
- router_weight: bfloat16 [1024, 16], P(('row', 'seq')), may hold values from -0.09375 to 0.09375
- gate_weight: bfloat16 [16, 1024, 512], P('row', 'seq'), may hold values from -0.1875 to 0.1875
- up_weight: bfloat16 [16, 1024, 512], P('row', 'seq'), may hold values from -0.1875 to 0.1875
- down_weight: bfloat16 [16, 512, 1024], P('row', None, 'seq'), may hold values from -0.75 to 0.75
Outputs:
- hidden_out: bfloat16 [4, 1024, 1024], P('row', 'seq')
- hidden_grad: bfloat16 [4, 1024, 1024], P('row', 'seq')
- attn_gaingrad: float32 [1024], P(('row', 'seq'))
- query_grad: float32 [1024, 1024], P(('row', 'seq'))
- key_grad: float32 [1024, 512], P(('row', 'seq'))
- value_grad: float32 [1024, 512], P(('row', 'seq'))
- out_grad: float32 [1024, 1024], P(None, ('row', 'seq'))
- ffn_gaingrad: float32 [1024], P(('row', 'seq'))
- router_grad: float32 [1024, 16], P(('row', 'seq'))
- gate_grad: float32 [16, 1024, 512], P('row', 'seq')
- up_grad: float32 [16, 1024, 512], P('row', 'seq')
- down_grad: float32 [16, 512, 1024], P('row', None, 'seq')
The draws below stay inside these ranges and needn't reach their ends.
Inputs may be any that keep to these rules, and one draw needn't show every extreme that they name: `segments`: in each row the ids never fall and run 0, 1, 2; segment 1 begins within the row's first 128 tokens but not at its first token, and ends within its last 128 tokens but before its last token. `routes`: the 8 experts of a token are all different. In each aligned block of 128 tokens of a packed row (that row's tokens on one device) no expert is named by more than 80 tokens, and in every draw some block has an expert named by exactly 80 tokens.
All inputs are finite; a program needn't handle non-finite values.
Results may differ from the reference program's by a relative error of at most 0.018.
Values may be sent and summed in bfloat16 or wider, within the bound.
No kernel may reach another device: no remote copies, remote signals or barrier semaphores. Data moves between devices by JAX's collectives and lax.ppermute only.
A program may use at most 256 MiB of HBM per device.

```python
import math
import jax
import jax.numpy as jnp
import numpy as np
from jax import lax

D = 1024
HEADS = 16
KV_HEADS = 8
HEAD_DIM = 64
FF = 512
TOP = 8
EXPERTS = 16
SPAN = 128
MOST = 80
LENGTH = 1024
ROWS = 4


def draw_segments(key, part):
    key = jax.random.fold_in(key, 11)
    first_key, last_key = jax.random.split(key)
    starts = jax.random.randint(first_key, (ROWS, 1), 1, SPAN)
    finishes = LENGTH - jax.random.randint(last_key, (ROWS, 1), 1, SPAN)
    position = jnp.arange(LENGTH, dtype=jnp.int32)[None, :]
    return (position >= starts).astype(jnp.int32) + (position >= finishes).astype(jnp.int32)


def with_spikes(values, key, source, target, blocks, factor):
    def block_of(dim):
        return (jnp.arange(values.shape[dim]) // (values.shape[dim] // blocks)).reshape((-1,) + (1,) * (values.ndim - 1 - dim))

    one_side = jax.random.permutation(key, blocks)[block_of(target)]
    other_side = (block_of(target) + blocks // 2) % blocks
    return jnp.where((block_of(source) == one_side) | (block_of(source) == other_side), factor * values, values)


def block_levels(rng, shape, cuts, least, largest):
    loudness, own = 1.0, jax.random.fold_in(rng, 6)
    for dim, parts in cuts:
        steps = jnp.exp(jax.random.uniform(jax.random.fold_in(own, dim), (parts,), jnp.float32, least / len(cuts), largest / len(cuts)))
        loudness = loudness * jnp.repeat(steps, shape[dim] // parts).reshape([-1 if axis == dim else 1 for axis in range(len(shape))])
    return loudness


def shared_out(own_key, own, number, rows, amount, top, reach, slope):
    sequence = jax.random.permutation(own_key, amount)
    crowded, usual = load_shares(amount, rows * top, reach, slope, True), load_shares(amount, rows * top, reach, slope, False)
    places = jnp.arange(amount)

    def named(lengths, offset_by):
        used = int((lengths > 0).sum())
        fixed = max(1, used // 4)
        passed = fixed + (places - fixed + offset_by * (used - fixed)) % max(1, amount - fixed)
        return jnp.zeros((amount,), jnp.int32).at[sequence[jnp.where(places < fixed, places, passed)]].set(jnp.asarray(lengths, jnp.int32))

    lengths = jnp.where(number % 4 == 0, named(crowded, number // 4), named(usual, number - number // 4 - 1))
    mixed = jax.random.permutation(jax.random.fold_in(own, 3), amount)
    giver, taker = mixed[0:amount // 2 * 2:2], mixed[1:amount // 2 * 2:2]
    room = jnp.minimum(lengths[giver] - 1, reach - lengths[taker]) // 2
    room = jnp.where((giver == sequence[0]) | (taker == sequence[0]) | (lengths[taker] == 0), 0, jnp.maximum(room, 0))
    passed = jax.random.randint(jax.random.fold_in(own, 4), (amount // 2,), 0, 1 << 20) % (room + 1)
    lengths = lengths.at[giver].add(-passed).at[taker].add(passed)
    labels = jnp.searchsorted(jnp.cumsum(lengths), jnp.arange(rows * top), side="right").astype(jnp.int32)
    listing = labels.reshape(top, rows).T
    listing = listing[jax.random.permutation(jax.random.fold_in(own, 1), rows)]
    offset_by = jax.random.randint(jax.random.fold_in(own, 2), (rows, 1), 0, top)
    return jnp.take_along_axis(listing, (jnp.arange(top)[None, :] + offset_by) % top, axis=1)


def load_shares(count, total, most, skew, full):
    portions = [(1 << 20) // math.isqrt(grade ** skew) + 1 for grade in range(1, count + 1)]
    largest = most if full else min(most, max(-(-total // count), total * portions[0] // sum(portions)))
    least = 1 if total - largest >= count - 1 else 0
    counts, spare = [largest] + [least] * (count - 1), total - largest - least * (count - 1)
    while spare > 0:
        free = [i for i in range(1, count) if counts[i] < largest] or [i for i in range(1, count) if counts[i] < most]
        whole, budget = sum([portions[i] for i in free]), spare
        for i in free:
            addition = min(most - counts[i], max(1, budget * portions[i] // whole), spare)
            counts[i] = counts[i] + addition
            spare = spare - addition
    return np.array(counts)


def centred(key, dims, scale, most, cuts=(), kind=jnp.bfloat16):
    result = jax.random.normal(key, dims, jnp.float32) * scale
    if len(cuts) > 0:
        result = block_levels(key, dims, cuts, -0.22, 0.18) * result
    return jnp.clip(result, min=-most, max=most).astype(kind)


def heavy_noise(own_key, extent, deviation, limit, shards, heavy, kind=jnp.bfloat16):
    entries = deviation * jax.random.normal(own_key, extent, jnp.float32)
    if shards:
        entries = entries * block_levels(own_key, extent, shards, -0.22, 0.18)
    return jnp.clip(with_spikes(entries, jax.random.fold_in(own_key, 3), *heavy), -limit, limit).astype(kind)


def setup_inputs(seed: int = 0) -> dict:
    key_list = jax.random.split(jax.random.key(seed), 15)
    hidden_in = centred(key_list[0], (ROWS, LENGTH, D), 1.0, 6.0, ((0, 4), (1, 8)))
    segments = draw_segments(jax.random.fold_in(key_list[14], 71), 0)
    routes_keys = jax.random.split(jax.random.fold_in(key_list[2], 1), ROWS * LENGTH // SPAN)
    routes_turns = jax.random.permutation(jax.random.fold_in(key_list[2], 3), ROWS * LENGTH // SPAN)
    routes = jax.vmap(lambda own, number: shared_out(jax.random.fold_in(key_list[2], 2), own, number, SPAN, EXPERTS, TOP, MOST, 2))(routes_keys, routes_turns).reshape((ROWS, LENGTH, TOP))
    cotangent = heavy_noise(key_list[3], (ROWS, LENGTH, D), 1.0, 6.0, ((0, 4), (1, 8)), (1, 2, 8, 2.0))
    attn_gain = jnp.clip(1.0 + 0.1 * jax.random.normal(key_list[4], (D,), jnp.float32), 0.5, 1.5).astype(jnp.bfloat16)
    query_weight = centred(key_list[5], (D, HEADS * HEAD_DIM), D ** -0.5, 0.1875, ((0, 32),))
    key_weight = centred(key_list[6], (D, KV_HEADS * HEAD_DIM), D ** -0.5, 0.1875, ((0, 32),))
    value_weight = centred(key_list[7], (D, KV_HEADS * HEAD_DIM), D ** -0.5, 0.1875, ((0, 32),))
    out_weight = centred(key_list[8], (HEADS * HEAD_DIM, D), (HEADS * HEAD_DIM // 16) ** -0.5, 0.75, ((1, 32),))
    ffn_gain = jnp.clip(1.0 + 0.1 * jax.random.normal(key_list[9], (D,), jnp.float32), 0.5, 1.5).astype(jnp.bfloat16)
    router_weight = centred(key_list[10], (D, EXPERTS), (4 * D) ** -0.5, 0.09375, ((0, 32),))
    gate_weight = centred(key_list[11], (EXPERTS, D, FF), D ** -0.5, 0.1875, ((0, 4), (1, 8)))
    up_weight = centred(key_list[12], (EXPERTS, D, FF), D ** -0.5, 0.1875, ((0, 4), (1, 8)))
    down_weight = centred(key_list[13], (EXPERTS, FF, D), (FF // 8) ** -0.5, 0.75, ((0, 4), (2, 8)))
    return {"hidden_in": hidden_in, "segments": segments, "routes": routes, "cotangent": cotangent, "attn_gain": attn_gain, "query_weight": query_weight, "key_weight": key_weight, "value_weight": value_weight, "out_weight": out_weight, "ffn_gain": ffn_gain, "router_weight": router_weight, "gate_weight": gate_weight, "up_weight": up_weight, "down_weight": down_weight}


EPS = 1e-06
THETA = 10000.0
NEG = -1e+30
HIGH = lax.Precision.HIGHEST

@jax.custom_vjp
def low(v):
    return lax.optimization_barrier(v.astype(jnp.bfloat16)).astype(jnp.float32)

@jax.custom_vjp
def low_back(v):
    return v

def low_keep(v):
    return (low(v), None)

def low_pass(kept, grad):
    return (grad,)

def back_keep(v):
    return (v, None)

def back_low(kept, grad):
    return (low(grad),)
low.defvjp(low_keep, low_pass)
low_back.defvjp(back_keep, back_low)

def matmul(left_side, right_side):
    return jnp.dot(left_side, right_side, precision=HIGH)

def rms_scale(inputs, gain_vec):
    inverse = lax.rsqrt(lax.optimization_barrier(jnp.mean(inputs * inputs, axis=-1, keepdims=True)) + EPS)
    return inputs * inverse * gain_vec

def rotate(values_in, cosine_part, sine_part):
    middle = values_in.shape[-1] // 2
    leading = values_in[..., :middle]
    trailing = values_in[..., middle:]
    return jnp.concatenate([leading * cosine_part - trailing * sine_part, trailing * cosine_part + leading * sine_part], axis=-1)

def slot_tables(routes, capacity, experts):
    block_total, block_len, choose = routes.shape
    onehot = (routes[..., None] == jnp.arange(experts, dtype=jnp.int32)).astype(jnp.int32)
    per_token = lax.optimization_barrier(jnp.sum(onehot, axis=2)).astype(jnp.int32)
    before = (jnp.cumsum(per_token, axis=1) - per_token).astype(jnp.int32)
    placed = jnp.take_along_axis(before, routes, axis=2).astype(jnp.int32)
    slot_ids = (routes * capacity + placed).astype(jnp.int32).reshape(block_total, block_len * choose)
    owners = jnp.repeat(jnp.arange(block_len, dtype=jnp.int32), choose)

    def fill_table(indices):
        return jnp.full((experts * capacity,), block_len, jnp.int32).at[indices].set(owners)
    return (slot_ids, jax.vmap(fill_table)(slot_ids))

def take_rows(source_rows, indices):

    def single(rows_here, pick_rows):
        return jnp.take(rows_here, pick_rows, axis=0)
    return jax.vmap(single)(source_rows, indices)

def row_forward(row_in, row_segs, row_routes, attn_gain, query_weight, key_weight, value_weight, out_weight, ffn_gain, router_weight, gate_weight, up_weight, down_weight):
    length = row_in.shape[0]
    groups = HEADS // KV_HEADS
    middle = HEAD_DIM // 2
    score_scale = HEAD_DIM ** (-0.5)
    position = jnp.arange(length, dtype=jnp.int32)
    starts = lax.optimization_barrier(jnp.sum((row_segs[None, :] < row_segs[:, None]).astype(jnp.int32), axis=1)).astype(jnp.int32)
    positions = (position - starts).astype(jnp.float32)
    frequency = THETA ** (-jnp.arange(middle, dtype=jnp.float32) * 2.0 / HEAD_DIM)
    angles = positions[:, None] * frequency
    cosines = jnp.cos(angles)
    sines = jnp.sin(angles)
    attn_in = low(rms_scale(row_in, attn_gain))
    query_pre = low_back(matmul(attn_in, query_weight))
    key_pre = low_back(matmul(attn_in, key_weight))
    value_low = low(low_back(matmul(attn_in, value_weight))).reshape(length, KV_HEADS, HEAD_DIM)
    query_rot = low(rotate(query_pre.reshape(length, KV_HEADS, groups, HEAD_DIM), cosines[:, None, None], sines[:, None, None]))
    key_rot = low(rotate(key_pre.reshape(length, KV_HEADS, HEAD_DIM), cosines[:, None], sines[:, None]))
    query_block = min(512, length)
    block_count = length // query_block

    def attend(block_args):
        block_query, block_index, block_segs = block_args
        scores = low_back(jnp.einsum('ckgd,jkd->kgcj', block_query, key_rot, precision=HIGH) * score_scale)
        allowed = (position[None, :] <= block_index[:, None]) & (row_segs[None, :] == block_segs[:, None])
        scores = jnp.where(allowed[None, None], scores, NEG)
        probability = low(jax.nn.softmax(scores, axis=-1))
        return jnp.einsum('kgcj,jkd->ckgd', probability, value_low, precision=HIGH)
    mix_full = lax.map(jax.checkpoint(attend), (query_rot.reshape(block_count, query_block, KV_HEADS, groups, HEAD_DIM), position.reshape(block_count, query_block), row_segs.reshape(block_count, query_block)))
    mix_low = low(low_back(mix_full.reshape(length, HEADS * HEAD_DIM)))
    residual = row_in + low_back(matmul(mix_low, out_weight))
    ffn_in = low(rms_scale(residual, ffn_gain))
    logits = low_back(matmul(ffn_in, router_weight))
    gate_probs = jax.nn.softmax(jnp.take_along_axis(logits, row_routes, axis=1), axis=-1)
    span_count = length // SPAN
    slot_ids, token_of = slot_tables(row_routes.reshape(span_count, SPAN, TOP), MOST, EXPERTS)
    padded = jnp.concatenate([ffn_in.reshape(span_count, SPAN, D), jnp.zeros((span_count, 1, D), jnp.float32)], axis=1)
    buffer = low_back(take_rows(padded, token_of).reshape(span_count, EXPERTS, MOST, D))
    gate_pre = low_back(jnp.einsum('bemd,edf->bemf', buffer, gate_weight, precision=HIGH))
    up_pre = low_back(jnp.einsum('bemd,edf->bemf', buffer, up_weight, precision=HIGH))
    hidden_act = low(jax.nn.silu(gate_pre) * up_pre)
    expert_out = low(low_back(jnp.einsum('bemf,efd->bemd', hidden_act, down_weight, precision=HIGH)))
    routed = take_rows(expert_out.reshape(span_count, EXPERTS * MOST, D), slot_ids).reshape(length, TOP, D)
    return residual + lax.optimization_barrier(jnp.sum(gate_probs[..., None] * routed, axis=1))

def reference(hidden_in, segments, routes, cotangent, attn_gain, query_weight, key_weight, value_weight, out_weight, ffn_gain, router_weight, gate_weight, up_weight, down_weight):
    weights = (attn_gain.astype(jnp.float32), query_weight.astype(jnp.float32), key_weight.astype(jnp.float32), value_weight.astype(jnp.float32), out_weight.astype(jnp.float32), ffn_gain.astype(jnp.float32), router_weight.astype(jnp.float32), gate_weight.astype(jnp.float32), up_weight.astype(jnp.float32), down_weight.astype(jnp.float32))

    def forward(inputs, params):

        def row_step(unused_state, row_args):
            row_in, row_segs, row_routes = row_args
            return (unused_state, jax.checkpoint(row_forward)(row_in, row_segs, row_routes, *params))
        return lax.scan(row_step, jnp.zeros((), jnp.float32), (inputs, segments, routes))[1]
    layer_sum, pullback = jax.vjp(forward, hidden_in.astype(jnp.float32), weights)
    input_slope, weight_slopes = pullback(cotangent.astype(jnp.float32))
    return (layer_sum.astype(jnp.bfloat16), input_slope.astype(jnp.bfloat16), weight_slopes[0], weight_slopes[1], weight_slopes[2], weight_slopes[3], weight_slopes[4], weight_slopes[5], weight_slopes[6], weight_slopes[7], weight_slopes[8], weight_slopes[9])
```

```python
import jax
import jax.numpy as jnp
from jax import lax
from jax.sharding import Mesh
from jax.sharding import PartitionSpec as P

HEADS = 16
KV_HEADS = 8
HEAD_DIM = 64

EPS = 1e-06
THETA = 10000.0
NEG = -1e30
GROUP = 4

BF = jnp.bfloat16
F32 = jnp.float32

SEQ = ("zh", "zl", "core")
DEPTH = ("zh", "zl")
ALL = ("row", "zh", "zl", "core")
TEAM = ("row", "zl")


def nt(left, right):
    return lax.dot_general(left, right, (((1,), (1,)), ((), ())), preferred_element_type=F32)


def nn(left, right):
    return lax.dot_general(left, right, (((1,), (0,)), ((), ())), preferred_element_type=F32)


def tn(left, right):
    return lax.dot_general(left, right, (((0,), (0,)), ((), ())), preferred_element_type=F32)


def pad_to(flat, size):
    return jnp.concatenate([flat, jnp.zeros((size - flat.shape[0],), flat.dtype)])


def rotate(values_in, cosines, sines):
    tokens, width = values_in.shape
    heads = values_in.reshape(tokens, width // HEAD_DIM, 2, HEAD_DIM // 2)
    first, second = heads[:, :, 0], heads[:, :, 1]
    cosines, sines = cosines[:, None], sines[:, None]
    turned = jnp.stack([first * cosines - second * sines, second * cosines + first * sines], axis=2)
    return turned.reshape(tokens, width)


def shards(
    hidden_in,
    segments,
    routes,
    cotangent,
    attn_gain,
    query_weight,
    key_weight,
    value_weight,
    out_weight,
    ffn_gain,
    router_weight,
    gate_weight,
    up_weight,
    down_weight,
):
    rows = lax.axis_size("row")
    far, near, cores = lax.axis_size("zh"), lax.axis_size("zl"), lax.axis_size("core")
    depth = far * near
    seqs = depth * cores
    span, width = hidden_in.shape[1:]
    length = span * seqs
    feats = query_weight.shape[0]
    experts = router_weight.shape[1]
    held, slab, hidden = gate_weight.shape
    mine = held // near
    heads = HEADS // seqs
    groups = HEADS // KV_HEADS
    key_heads = max(1, heads // groups)
    query_cols, key_cols = heads * HEAD_DIM, key_heads * HEAD_DIM
    cols = query_cols + 2 * key_cols
    scale = HEAD_DIM**-0.5

    own = hidden_in[0]
    row_hidden = lax.all_gather(own, SEQ, axis=0, tiled=True)

    def key_start(place):
        return (place * heads // groups) * HEAD_DIM

    query_part = query_weight.reshape(feats, seqs, query_cols)
    key_part = jnp.stack([key_weight[:, key_start(s) : key_start(s) + key_cols] for s in range(seqs)], 1)
    value_part = jnp.stack([value_weight[:, key_start(s) : key_start(s) + key_cols] for s in range(seqs)], 1)
    dense = jnp.concatenate([query_part, key_part, value_part], axis=2).transpose(1, 0, 2)
    small_len = 2 * feats + span + feats * experts
    small_rows = -(-small_len // cols)
    small = pad_to(
        jnp.concatenate([attn_gain, ffn_gain, segments[0].astype(BF), router_weight.reshape(-1)]),
        small_rows * cols,
    ).reshape(small_rows, cols)
    packed = jnp.concatenate([dense, jnp.broadcast_to(small, (seqs, small_rows, cols))], axis=1)
    packed = jnp.broadcast_to(packed, (rows, seqs, feats + small_rows, cols))
    packed = lax.all_to_all(
        packed.reshape(rows * seqs, feats + small_rows, cols), ALL, 0, 0, tiled=True
    )
    proj = packed[:, :feats].reshape(width, cols)
    small = packed[:, feats:].reshape(rows * seqs, -1)
    gain_one = small[:, :feats].reshape(width).astype(F32)
    gain_two = small[:, feats : 2 * feats].reshape(width).astype(F32)
    segs_all = small[:, 2 * feats : 2 * feats + span].reshape(rows, length)
    row_segs = lax.dynamic_index_in_dim(segs_all, lax.axis_index("row"), 0, False).astype(jnp.int32)
    router_full = small[:, 2 * feats + span : small_len].reshape(width, experts)

    out_full = lax.all_gather(out_weight.T, ALL, axis=0, tiled=True)
    upstream_team = lax.all_gather(cotangent[0], TEAM, axis=0, tiled=True)

    stacked = jnp.stack([gate_weight, up_weight, down_weight.transpose(0, 2, 1)])
    stacked = stacked.reshape(3, near, mine, slab, hidden).transpose(1, 0, 2, 3, 4)
    stacked = jnp.broadcast_to(stacked, (far, near, 3, mine, slab, hidden))
    stacked = lax.all_to_all(
        stacked.reshape(depth, 3, mine, slab, hidden), DEPTH, 0, 0, tiled=True
    )
    stacked = lax.all_gather(stacked, "core", axis=0, tiled=False)
    stacked = stacked.transpose(2, 3, 1, 0, 4, 5).reshape(3, mine, width, hidden)

    index = jnp.arange(length, dtype=jnp.int32)
    below_one = jnp.sum((row_segs < 1).astype(jnp.int32))
    below_two = jnp.sum((row_segs < 2).astype(jnp.int32))
    starts = jnp.where(row_segs == 0, 0, jnp.where(row_segs == 1, below_one, below_two))
    positions = (index - starts).astype(F32)
    frequency = THETA ** (-jnp.arange(HEAD_DIM // 2, dtype=F32) * 2.0 / HEAD_DIM)
    angles = positions[:, None] * frequency
    cosines, sines = jnp.cos(angles), jnp.sin(angles)
    row_f = row_hidden.astype(F32)
    row_inv = lax.rsqrt(jnp.mean(row_f * row_f, axis=-1, keepdims=True) + EPS)
    attn_in = (row_f * row_inv * gain_one).astype(BF)
    pre = nn(attn_in, proj)
    query_rot = rotate(pre[:, :query_cols], cosines, sines).astype(BF)
    key_rot = rotate(pre[:, query_cols : query_cols + key_cols], cosines, sines).astype(BF)
    value_low = pre[:, query_cols + key_cols :].astype(BF)
    allowed = (index[None, :] <= index[:, None]) & (row_segs[:, None] == row_segs[None, :])

    def head(array, number):
        return array[:, number * HEAD_DIM : (number + 1) * HEAD_DIM]

    kept, mixes = [], []
    for number in range(heads):
        kv = number // groups
        scores = nt(head(query_rot, number), head(key_rot, kv)) * scale
        scores = jnp.where(allowed, scores, NEG)
        top = jnp.max(scores, axis=-1, keepdims=True)
        raised = jnp.exp(scores - top)
        probs = raised / jnp.sum(raised, axis=-1, keepdims=True)
        kept.append(probs)
        mixes.append(nn(probs.astype(BF), head(value_low, kv)))
    mix_full = jnp.concatenate(mixes, axis=1)
    mix_low = lax.all_to_all(
        mix_full.astype(BF).reshape(seqs, span, query_cols), SEQ, 0, 0, tiled=True
    )
    mix_low = mix_low.transpose(1, 0, 2).reshape(span, width)

    own_f = own.astype(F32)
    residual = own_f + nt(mix_low, out_full)
    inv_two = lax.rsqrt(jnp.mean(residual * residual, axis=-1, keepdims=True) + EPS)
    ffn_in = (residual * inv_two * gain_two).astype(BF)
    logits = nn(ffn_in, router_full)
    named = jnp.any(routes[0][:, :, None] == jnp.arange(experts, dtype=jnp.int32), axis=1)
    logits = jnp.where(named, logits, NEG)
    raised = jnp.where(named, jnp.exp(logits - jnp.max(logits, axis=-1, keepdims=True)), 0.0)
    gates = raised / jnp.sum(raised, axis=-1, keepdims=True)
    gates_high = gates.astype(BF)
    gates_rest = (gates - gates_high.astype(F32)).astype(BF)
    extra = jnp.concatenate(
        [gates_high, gates_rest, jnp.zeros((span, 128 - 2 * experts), BF)], axis=1
    )
    team = lax.all_gather(jnp.concatenate([ffn_in, extra], axis=1), TEAM, axis=0, tiled=True)

    team_in = team[:, :width]
    team_up = upstream_team.astype(F32)
    first_expert = lax.axis_index("row") * held + lax.axis_index("zl") * mine
    grads = []
    out_sum, slope_sum, slope_cols = 0.0, 0.0, 0.0
    for number in range(mine):
        lane = (jnp.arange(experts) == first_expert + number).astype(F32)
        gate = jnp.sum(
            (
                team[:, width : width + experts].astype(F32)
                + team[:, width + experts : width + 2 * experts].astype(F32)
            )
            * lane,
            axis=1,
            keepdims=True,
        )
        gate_w, up_w, down_w = stacked[0, number], stacked[1, number], stacked[2, number]
        gate_pre = nn(team_in, gate_w)
        up_pre = nn(team_in, up_w)
        sigmoid = jax.nn.sigmoid(gate_pre)
        act = (gate_pre * sigmoid * up_pre).astype(BF)
        expert_out = nt(act, down_w)
        routed_slope = (gate * team_up).astype(BF)
        gate_slope = jnp.sum(team_up * expert_out, axis=1, keepdims=True)
        out_sum = out_sum + gate * expert_out
        hidden_slope = nn(routed_slope, down_w)
        down_grad = tn(routed_slope, act)
        gate_low = (hidden_slope * up_pre * sigmoid * (1.0 + gate_pre * (1.0 - sigmoid))).astype(BF)
        up_low = (hidden_slope * gate_pre * sigmoid).astype(BF)
        gate_grad = tn(team_in, gate_low)
        up_grad = tn(team_in, up_low)
        slope_sum = slope_sum + nt(gate_low, gate_w) + nt(up_low, up_w)
        slope_cols = slope_cols + gate_slope * lane
        grads.append(jnp.stack([gate_grad, up_grad, down_grad]))
    slope_send = jnp.concatenate(
        [
            slope_sum.astype(BF),
            slope_cols.astype(BF),
            jnp.zeros((slope_sum.shape[0], 128 - experts), BF),
        ],
        axis=1,
    )

    def to_owners(partial):
        wide = partial.shape[1]
        step = lax.all_to_all(
            partial.reshape(rows, near * span, wide), "row", 0, 0, tiled=True
        )
        step = jnp.sum(step.astype(F32), axis=0).astype(BF)
        step = lax.all_to_all(step.reshape(near, span, wide), "zl", 0, 0, tiled=True)
        return jnp.sum(step.astype(F32), axis=0)

    slope_back = to_owners(slope_send)
    hidden_out = (residual + to_owners(out_sum.astype(BF))).astype(BF)

    grads = jnp.stack(grads, axis=1).astype(BF)
    grads = grads.reshape(3, mine, depth, cores, slab, hidden).transpose(3, 2, 0, 1, 4, 5)
    grads = lax.all_to_all(grads, "core", 0, 0, tiled=True)
    grads = jnp.sum(grads.astype(F32), axis=0).astype(BF)
    grads = lax.all_to_all(grads, DEPTH, 0, 0, tiled=True)
    grads = grads.reshape(far, near, 3, mine, slab, hidden).astype(F32).sum(axis=0)
    grads = grads.transpose(1, 0, 2, 3, 4).reshape(3, held, slab, hidden)

    token_slope = slope_back[:, :width]
    gate_slope = slope_back[:, width : width + experts]
    logit_slope = (
        gates * (gate_slope - jnp.sum(gates * gate_slope, axis=-1, keepdims=True))
    ).astype(BF)
    router_part = tn(ffn_in, logit_slope)
    ffn_slope = token_slope + nt(logit_slope, router_full)
    upstream = cotangent[0].astype(F32)
    scaled_two = ffn_slope * gain_two
    ffn_gain_part = jnp.sum(ffn_slope * residual * inv_two, axis=0)
    resid_slope = (
        upstream
        + inv_two * scaled_two
        - residual * inv_two**3 * jnp.mean(scaled_two * residual, axis=-1, keepdims=True)
    )
    branch_low = resid_slope.astype(BF)
    out_part = tn(branch_low, mix_low).astype(BF)
    out_part = lax.psum_scatter(out_part, "row", scatter_dimension=0, tiled=True)
    out_grad = lax.psum_scatter(out_part, SEQ, scatter_dimension=0, tiled=True)
    mix_slope = nn(branch_low, out_full).astype(BF)
    mix_slope = mix_slope.reshape(span, seqs, query_cols).transpose(1, 0, 2)
    mix_slope = lax.all_to_all(mix_slope, SEQ, 0, 0, tiled=True).reshape(length, query_cols)

    query_acc, key_acc, value_acc = [], [0.0] * key_heads, [0.0] * key_heads
    for number in range(heads):
        kv = number // groups
        probs, slope = kept[number], head(mix_slope, number)
        delta = jnp.sum(slope.astype(F32) * mixes[number], axis=-1, keepdims=True)
        prob_slope = nt(slope, head(value_low, kv))
        score_low = (probs * (prob_slope - delta)).astype(BF)
        value_acc[kv] = value_acc[kv] + tn(probs.astype(BF), slope)
        query_acc.append(nn(score_low, head(key_rot, kv)) * scale)
        key_acc[kv] = key_acc[kv] + tn(score_low, head(query_rot, number)) * scale
    lows = jnp.concatenate(
        [
            rotate(jnp.concatenate(query_acc, axis=1), cosines, -sines),
            rotate(jnp.concatenate(key_acc, axis=1), cosines, -sines),
            jnp.concatenate(value_acc, axis=1),
        ],
        axis=1,
    ).astype(BF)
    proj_part = tn(attn_in, lows)
    attn_gain_part = jnp.sum(proj_part * proj.astype(F32), axis=1) / gain_one
    attn_slope = nt(lows, proj).astype(BF)
    attn_slope = lax.psum_scatter(attn_slope, SEQ, scatter_dimension=0, tiled=True).astype(F32)

    blocks = rows * seqs
    send_small = jnp.concatenate(
        [
            attn_gain_part.reshape(blocks, feats),
            ffn_gain_part.reshape(blocks, feats),
            router_part.reshape(blocks, feats * experts),
        ],
        axis=1,
    )
    back_len = send_small.shape[1]
    back_rows = -(-back_len // cols)
    send_small = jnp.concatenate(
        [send_small, jnp.zeros((blocks, back_rows * cols - back_len), F32)], axis=1
    ).reshape(blocks, back_rows, cols)
    send = jnp.concatenate([proj_part.reshape(blocks, feats, cols), send_small], axis=1).astype(BF)
    back = lax.all_to_all(send, ALL, 0, 0, tiled=True).astype(F32)
    small_back = jnp.sum(back[:, feats:], axis=0).reshape(-1)
    attn_gain_grad = small_back[:feats]
    ffn_gain_grad = small_back[feats : 2 * feats]
    router_grad = small_back[2 * feats : back_len].reshape(feats, experts)
    proj_back = jnp.sum(back[:, :feats].reshape(rows, seqs, feats, cols), axis=0)
    query_grad = proj_back[:, :, :query_cols].transpose(1, 0, 2).reshape(feats, HEADS * HEAD_DIM)

    def key_grads(part):
        share = seqs * key_heads // KV_HEADS
        part = part.reshape(seqs // share, share, feats, key_cols).sum(axis=1)
        return part.transpose(1, 0, 2).reshape(feats, KV_HEADS * HEAD_DIM)

    key_grad = key_grads(proj_back[:, :, query_cols : query_cols + key_cols])
    value_grad = key_grads(proj_back[:, :, query_cols + key_cols :])

    inv_one = lax.rsqrt(jnp.mean(own_f * own_f, axis=-1, keepdims=True) + EPS)
    scaled_one = attn_slope * gain_one
    hidden_grad = (
        resid_slope
        + inv_one * scaled_one
        - own_f * inv_one**3 * jnp.mean(scaled_one * own_f, axis=-1, keepdims=True)
    ).astype(BF)
    return (
        hidden_out[None],
        hidden_grad[None],
        attn_gain_grad,
        query_grad,
        key_grad,
        value_grad,
        out_grad.astype(F32).T,
        ffn_gain_grad,
        router_grad,
        grads[0],
        grads[1],
        grads[2].transpose(0, 2, 1),
    )


def solution(mesh):
    rows, seqs = mesh.shape["row"], mesh.shape["seq"]
    depth = seqs // 2
    held = 16 // rows
    near = min(GROUP, held, depth)
    fine = Mesh(mesh.devices.reshape(rows, depth // near, near, 2), ALL)
    token = P("row", SEQ, None)
    return jax.shard_map(
        shards,
        mesh=fine,
        in_specs=(
            token,
            P("row", SEQ),
            token,
            token,
            P(ALL),
            P(ALL, None),
            P(ALL, None),
            P(ALL, None),
            P(None, ALL),
            P(ALL),
            P(ALL, None),
            token,
            token,
            P("row", None, SEQ),
        ),
        out_specs=(
            token,
            token,
            P(ALL),
            P(ALL, None),
            P(ALL, None),
            P(ALL, None),
            P(None, ALL),
            P(ALL),
            P(ALL, None),
            token,
            token,
            P("row", None, SEQ),
        ),
        check_vma=False,
    )
```

```python
import functools

import jax
import jax.numpy as jnp
import numpy as np
from jax import lax
from jax.experimental import pallas as pl
from jax.experimental.pallas import tpu as pltpu
from jax.sharding import Mesh
from jax.sharding import PartitionSpec as P

HEADS = 16
KV_HEADS = 8
HEAD_DIM = 64
HALF = HEAD_DIM // 2

EPS = 1e-06
THETA = 10000.0
NEG = -1e30
GROUP = 2
LANES = 128
TILE = 16
COUNTS = 160
QUERIES = 256
CHUNK = 256
VMEM_BYTES = 60 * 1024 * 1024

BF = jnp.bfloat16
F32 = jnp.float32

SEQ = ("zh", "zl", "core")
DEPTH = ("zh", "zl")
ALL = ("row", "zh", "zl", "core")
TEAM = ("row", "zl")

SMEM = pl.BlockSpec(memory_space=pltpu.SMEM)
VMEM = pl.BlockSpec(memory_space=pltpu.VMEM)
ANY = pl.BlockSpec(memory_space=pl.ANY)


def nt(left, right):
    return lax.dot_general(left, right, (((1,), (1,)), ((), ())), preferred_element_type=F32)


def nn(left, right):
    return lax.dot_general(left, right, (((1,), (0,)), ((), ())), preferred_element_type=F32)


def tn(left, right):
    return lax.dot_general(left, right, (((0,), (0,)), ((), ())), preferred_element_type=F32)


def shape(dims, kind):
    return jax.ShapeDtypeStruct(dims, kind)


def run(kernel, name, out_shape, in_specs, args, micros, scratch=()):
    return pl.pallas_call(
        kernel,
        out_shape=out_shape,
        in_specs=in_specs,
        out_specs=jax.tree.map(lambda _: VMEM, out_shape),
        scratch_shapes=list(scratch),
        compiler_params=pltpu.CompilerParams(vmem_limit_bytes=VMEM_BYTES),
        cost_estimate=pl.CostEstimate(
            flops=int(micros * 1e9), bytes_accessed=1024, transcendentals=0
        ),
        name=name,
    )(*args)


def after(value, *earlier):
    return lax.optimization_barrier((value, *earlier))[0]


def tie(*values):
    return lax.optimization_barrier(values)


def swap(block, axes, mask):
    return lax.ppermute(block, axes, [(i, i ^ mask) for i in range(lax.axis_size(axes))])


def masked(block, axes):
    return [swap(block, axes, mask) if mask else block for mask in range(lax.axis_size(axes))]


def pack_kernel(seqs, query_cols, key_cols, starts, place, query, key, value, router, gain_one, gain_two, segs, out, wide):
    feats = query.shape[0]
    room = out.shape[1] - TILE
    cols = out.shape[2]
    mine = place[3]
    row = lax.broadcasted_iota(jnp.int32, (TILE, LANES), 0)
    lane = lax.broadcasted_iota(jnp.int32, (TILE, LANES), 1)
    times = LANES // feats
    one = jnp.concatenate([gain_one[...].astype(F32)] * times, axis=1)
    two = jnp.concatenate([gain_two[...].astype(F32)] * times, axis=1)
    slot = (row % 8) * times + lane // feats
    gains = jnp.where(slot == mine, jnp.where(row < 8, one, two), 0.0)
    ids = segs[...]
    below_one = jnp.sum((ids < 1).astype(F32), axis=1, keepdims=True)
    below_two = jnp.sum((ids < 2).astype(F32), axis=1, keepdims=True)
    side = lax.broadcasted_iota(jnp.int32, (TILE, HALF), 0)
    counts = jnp.where(side == 0, below_one, jnp.where(side == 1, below_two, 0.0))
    small = [gains, router[...].astype(F32)]
    if feats < HALF:
        small.append(jnp.zeros((TILE, HALF - feats), F32))
    small.append(counts)
    if cols > COUNTS + HALF:
        small.append(jnp.zeros((TILE, cols - COUNTS - HALF), F32))
    small = jnp.concatenate(small, axis=1).astype(BF)
    for number in range(seqs):
        first = starts[number]
        block = jnp.concatenate(
            [
                query[:, number * query_cols : (number + 1) * query_cols].astype(F32),
                key[:, first : first + key_cols].astype(F32),
                value[:, first : first + key_cols].astype(F32),
            ],
            axis=1,
        )
        wide[:, number * cols : (number + 1) * cols] = block.astype(BF)
        if room > feats:
            block = jnp.concatenate([block, jnp.zeros((room - feats, cols), F32)], axis=0)
        out[number, :room] = block.astype(BF)
        out[number, room:] = small


def full_gain(small, first):
    total = jnp.sum(small[:, first : first + 8, :LANES].astype(F32), axis=0)
    return jnp.concatenate([total[i : i + 1] for i in range(8)], axis=1)


def attend_kernel(heads, key_heads, scale, place, freq, proj, small, *refs):
    parts = refs[:-6]
    attn_in, rotated, turns, probs, mix_full, mix_send = refs[-6:]
    span = parts[0].shape[0]
    length = attn_in.shape[0]
    seqs = len(parts)
    gain = full_gain(small[...], 0)
    for number, part in enumerate(parts):
        mask, core = number // 2, number % 2
        spot = (place[1] ^ mask) * 2 + (place[2] ^ core)
        block = part[...].astype(F32)
        inverse = lax.rsqrt(jnp.mean(block * block, axis=-1, keepdims=True) + EPS)
        attn_in[pl.ds(pl.multiple_of(spot * span, span), span), :] = (block * inverse * gain).astype(BF)
    counts = jnp.sum(small[pl.ds(place[0] * seqs, seqs)].astype(F32), axis=0)
    below_one = counts[0:1, COUNTS : COUNTS + 1].astype(jnp.int32)
    below_two = counts[1:2, COUNTS : COUNTS + 1].astype(jnp.int32)
    index = lax.broadcasted_iota(jnp.int32, (length, 1), 0)
    start = jnp.where(index >= below_two, below_two, jnp.where(index >= below_one, below_one, 0))
    angles = (index - start).astype(F32) * freq[...]
    cosine, sine = jnp.cos(angles), jnp.sin(angles)
    turns[...] = jnp.concatenate([cosine, sine], axis=1)
    pre = nn(attn_in[...], proj[...])

    def turned(number):
        first = pre[:, number * HEAD_DIM : number * HEAD_DIM + HALF]
        second = pre[:, number * HEAD_DIM + HALF : (number + 1) * HEAD_DIM]
        return [first * cosine - second * sine, second * cosine + first * sine]

    pieces = []
    for number in range(heads + key_heads):
        pieces += turned(number)
    pieces.append(pre[:, (heads + key_heads) * HEAD_DIM :])
    rotated[...] = jnp.concatenate(pieces, axis=1).astype(BF)
    groups = heads // key_heads
    for number in range(heads):
        kv = number // groups
        key_at = (heads + kv) * HEAD_DIM
        value_at = (heads + key_heads + kv) * HEAD_DIM
        for first in range(0, length, QUERIES):
            rows = slice(first, first + QUERIES)
            keys = first + QUERIES
            query = rotated[rows, number * HEAD_DIM : (number + 1) * HEAD_DIM]
            scores = nt(query, rotated[:keys, key_at : key_at + HEAD_DIM]) * scale
            column = lax.broadcasted_iota(jnp.int32, (QUERIES, keys), 1)
            allowed = (column <= index[rows]) & (column >= start[rows])
            scores = jnp.where(allowed, scores, NEG)
            raised = jnp.exp(scores - jnp.max(scores, axis=-1, keepdims=True))
            weight = (raised / jnp.sum(raised, axis=-1, keepdims=True)).astype(BF)
            probs[number, rows, :keys] = weight
            mix = nn(weight, rotated[:keys, value_at : value_at + HEAD_DIM])
            mix_full[rows, number * HEAD_DIM : (number + 1) * HEAD_DIM] = mix
    for number in range(seqs):
        mix_send[number] = mix_full[number * span : (number + 1) * span].astype(BF)


def put_pieces(place, target, halves):
    for core, half in enumerate(halves):
        for mask in range(half.shape[0]):
            for deep in range(half.shape[1]):
                spot = ((place[0] ^ mask) * half.shape[1] + (place[1] ^ deep)) * 2 + (place[2] ^ core)
                feats = half.shape[2]
                target[pl.ds(pl.multiple_of(spot * feats, feats), feats), :] = half[mask, deep]


def norm_kernel(experts, place, mix, own, small, router, routes, half_one, half_two, residual, mix_low, ffn_in, gates, send, out_full):
    span, width = own.shape
    put_pieces(place, out_full, (half_one, half_two))
    mix_low[...] = jnp.concatenate([mix[number] for number in range(mix.shape[0])], axis=1)
    total = own[...].astype(F32) + nt(mix_low[...], out_full[...])
    residual[...] = total
    inverse = lax.rsqrt(jnp.mean(total * total, axis=-1, keepdims=True) + EPS)
    normed = (total * inverse * full_gain(small[...], 8)).astype(BF)
    ffn_in[...] = normed
    logits = nt(normed, router[...])
    number = lax.broadcasted_iota(jnp.int32, (span, experts), 1)
    named = number < 0
    for choice in range(routes.shape[1]):
        named = named | (routes[:, choice : choice + 1] == number)
    logits = jnp.where(named, logits, NEG)
    raised = jnp.where(named, jnp.exp(logits - jnp.max(logits, axis=-1, keepdims=True)), 0.0)
    shares = raised / jnp.sum(raised, axis=-1, keepdims=True)
    gates[...] = shares
    high = shares.astype(BF).astype(F32)
    extra = jnp.concatenate(
        [high, shares - high, jnp.zeros((span, LANES - 2 * experts), F32)], axis=1
    ).astype(BF)
    send[:, :width] = normed
    send[:, width:] = extra


def expert_gate(team, rows, width, experts, expert):
    lane = (lax.broadcasted_iota(jnp.int32, (1, experts), 1) == expert).astype(F32)
    extra = team[rows, width : width + LANES].astype(F32)
    gate = (extra[:, :experts] + extra[:, experts : 2 * experts]) * lane
    return jnp.sum(gate, axis=1, keepdims=True)


def gather_slabs(place, pairs, targets, begin):
    kinds = [(pair, kind) for pair in pairs for kind in range(pair[0].shape[1])]
    for (pair, kind), target in zip(kinds, targets):
        depth, _, _, slab, _ = pair[0].shape
        for core, part in enumerate(pair):
            for mask in range(depth):
                spot = (place[1] ^ mask) * 2 + (place[2] ^ core)
                rows = pl.ds(pl.multiple_of(spot * slab, slab), slab)
                begin(part.at[mask, kind], target.at[:, rows, :])


def copier(sems):
    copies = []

    def begin(source, target):
        copy = pltpu.make_async_copy(source, target, sems.at[len(copies)])
        copy.start()
        copies.append(copy)

    return copies, begin


def rise_kernel(count, low, place, *refs):
    team_parts, up_parts, slabs = refs[:count], refs[count : 2 * count], refs[2 * count : 2 * count + 4]
    team, upstream, act, gate_pres, up_pres, gate_w, up_w, sems = refs[2 * count + 4 :]
    span, width = up_parts[0].shape[1:]
    mine = act.shape[0]
    copies, begin = copier(sems)
    for number in range(count):
        rows = pl.ds(number * span, span)
        begin(team_parts[number], team.at[rows, :])
        begin(up_parts[number].at[low], upstream.at[rows, :])
    gather_slabs(place, (slabs[:2], slabs[2:]), (gate_w, up_w), begin)
    for copy in copies:
        copy.wait()

    def step(number, carry):
        rows = pl.ds(pl.multiple_of(number * CHUNK, CHUNK), CHUNK)
        inputs = team[rows, :width]
        for place_here in range(mine):
            gate_pre = nn(inputs, gate_w[place_here])
            up_pre = nn(inputs, up_w[place_here])
            sigmoid = 1.0 / (1.0 + jnp.exp(-gate_pre))
            act[place_here, rows, :] = (gate_pre * sigmoid * up_pre).astype(BF)
            gate_pres[place_here, rows, :] = gate_pre.astype(BF)
            up_pres[place_here, rows, :] = up_pre.astype(BF)
        return carry

    lax.fori_loop(0, count * span // CHUNK, step, 0)


def fall_kernel(count, held, experts, place, team, upstream, act, gate_pres, up_pres, *refs):
    slabs, slope_parts = refs[:6], refs[6 : 6 + count]
    out, gate_low, up_low, slopes, outs, gate_w, up_w, down_w, sems = refs[6 + count :]
    tokens, width = upstream.shape
    span = tokens // count
    mine = act.shape[0]
    copies, begin = copier(sems)
    gather_slabs(place, (slabs[:2], slabs[2:4], slabs[4:]), (gate_w, up_w, down_w), begin)
    for copy in copies:
        copy.wait()

    def step(number, carry):
        rows = pl.ds(pl.multiple_of(number * CHUNK, CHUNK), CHUNK)
        up_f = upstream[rows, :].astype(F32)
        out_sum = jnp.zeros((CHUNK, width), F32)
        slope_sum = jnp.zeros((CHUNK, width), F32)
        columns = jnp.zeros((CHUNK, LANES), F32)
        for place_here in range(mine):
            expert = place[0] * held + place[4] * mine + place_here
            gate = expert_gate(team, rows, width, experts, expert)
            expert_out = nt(act[place_here, rows, :], down_w[place_here])
            out_sum = out_sum + gate * expert_out
            score = jnp.sum(up_f * expert_out, axis=1, keepdims=True)
            lane = lax.broadcasted_iota(jnp.int32, (1, LANES), 1)
            columns = jnp.where(lane == expert, score, columns)
            hidden_slope = nn((gate * up_f).astype(BF), down_w[place_here])
            gate_pre = gate_pres[place_here, rows, :].astype(F32)
            up_pre = up_pres[place_here, rows, :].astype(F32)
            sigmoid = 1.0 / (1.0 + jnp.exp(-gate_pre))
            gate_slope = hidden_slope * up_pre * sigmoid * (1.0 + gate_pre * (1.0 - sigmoid))
            gate_slope = gate_slope.astype(BF)
            up_slope = (hidden_slope * gate_pre * sigmoid).astype(BF)
            gate_low[place_here, rows, :] = gate_slope
            up_low[place_here, rows, :] = up_slope
            slope_sum = slope_sum + nt(gate_slope, gate_w[place_here])
            slope_sum = slope_sum + nt(up_slope, up_w[place_here])
        slopes[rows, :width] = slope_sum.astype(BF)
        slopes[rows, width:] = columns.astype(BF)
        outs[rows, :] = out_sum.astype(BF)
        return carry

    lax.fori_loop(0, tokens // CHUNK, step, 0)
    for number in range(count):
        rows = slice(number * span, (number + 1) * span)
        slope_parts[number][...] = slopes[rows, :]
        out[place[0] ^ number] = outs[rows, :]


def spread_grad(place, total, kind, number, ours, theirs):
    slab = ours.shape[3]
    for mask in range(ours.shape[0]):
        for core, target in ((0, ours), (1, theirs)):
            spot = (place[1] ^ mask) * 2 + (place[2] ^ core)
            block = total[pl.ds(pl.multiple_of(spot * slab, slab), slab), :]
            target[mask, kind, number] = block.astype(BF)


def down_kernel(halves, held, experts, place, *refs):
    groups = [refs[3 * number : 3 * number + 3] for number in range(halves)]
    ours, theirs, total = refs[3 * halves :]
    mine = groups[0][2].shape[0]
    width = groups[0][1].shape[1]
    for place_here in range(mine):
        expert = place[0] * held + place[4] * mine + place_here
        for number, (team, upstream, act) in enumerate(groups):
            gate = expert_gate(team, slice(None), width, experts, expert)
            grad = tn((gate * upstream[...].astype(F32)).astype(BF), act[place_here])
            if number == 0:
                total[...] = grad
            else:
                total[...] += grad
        spread_grad(place, total, 0, place_here, ours, theirs)


def weight_kernel(halves, place, *refs):
    groups = [refs[3 * number : 3 * number + 3] for number in range(halves)]
    ours, theirs, total = refs[3 * halves :]
    mine = groups[0][1].shape[0]
    width = total.shape[0]
    for kind in range(2):
        for place_here in range(mine):
            for number, (team, *lows) in enumerate(groups):
                grad = tn(team[:, :width], lows[kind][place_here])
                if number == 0:
                    total[...] = grad
                else:
                    total[...] += grad
            spread_grad(place, total, kind, place_here, ours, theirs)


def join_kernel(ours, others, *outs):
    depth = ours.shape[0]
    for number, out in enumerate(outs):
        kind, mask = number // depth, number % depth
        out[...] = (ours[mask, kind].astype(F32) + others[mask, kind].astype(F32)).astype(BF)


def share_kernel(near, place, *refs):
    parts, outs = refs[:-3], refs[-3:]
    depth = len(parts) // 3
    mine = parts[0].shape[0]
    for low in range(near):
        owner = place[4] ^ low
        for number in range(mine):
            for kind, out in enumerate(outs):
                of_kind = parts[kind * depth : (kind + 1) * depth]
                total = sum(part[number].astype(F32) for part in of_kind[low::near])
                out[owner * mine + number] = total if kind < 2 else total.T


def add_kernel(*refs):
    total = refs[0][...].astype(F32)
    for part in refs[1:-1]:
        total = total + part[...].astype(F32)
    refs[-1][...] = total.astype(BF)


def sum_kernel(residual, *refs):
    total = residual[...]
    for part in refs[:-1]:
        total = total + part[...].astype(F32)
    refs[-1][...] = total.astype(BF)


def back_kernel(cotangent, residual, ffn_in, gates, router, small, out_full, mix_low, *refs):
    slopes, (resid_slope, mix_send, out_part) = refs[:-3], refs[-3:]
    span, width = residual.shape
    experts = gates.shape[1]
    back = slopes[0][...].astype(F32)
    for part in slopes[1:]:
        back = back + part[...].astype(F32)
    scores = back[:, width : width + experts]
    shares = gates[...]
    logit_slope = shares * (scores - jnp.sum(shares * scores, axis=-1, keepdims=True))
    logit_slope = logit_slope.astype(BF)
    total = residual[...]
    inverse = lax.rsqrt(jnp.mean(total * total, axis=-1, keepdims=True) + EPS)
    ffn_slope = back[:, :width] + nn(logit_slope, router[...])
    scaled = ffn_slope * full_gain(small[...], 8)
    slope = (
        cotangent[...].astype(F32)
        + inverse * scaled
        - total * (inverse * inverse * inverse) * jnp.mean(scaled * total, axis=-1, keepdims=True)
    )
    resid_slope[...] = slope
    low = slope.astype(BF)
    mix_slope = nn(low, out_full[...]).astype(BF)
    cols = width // mix_send.shape[0]
    for number in range(mix_send.shape[0]):
        mix_send[number] = mix_slope[:, number * cols : (number + 1) * cols]
    out_part[:, :width] = tn(low, mix_low[...]).astype(BF)
    router_part = tn(ffn_in[...], logit_slope)
    gain_part = jnp.sum((ffn_slope * total * inverse).T, axis=1, keepdims=True)
    out_part[:, width:] = jnp.concatenate(
        [router_part, gain_part, jnp.zeros((width, LANES - experts - 1), F32)], axis=1
    ).astype(BF)


def attend_back_kernel(heads, key_heads, scale, place, slopes, probs, rotated, mix_full, turns, attn_in, proj, lows_send, *refs):
    row_parts, (lows, key_sum, value_sum, part) = refs[:-4], refs[-4:]
    length, width = attn_in.shape
    seqs, span, cols = lows_send.shape
    cosine, sine = turns[:, :HALF], turns[:, HALF:]
    groups = heads // key_heads
    key_sum[...] = jnp.zeros_like(key_sum)
    value_sum[...] = jnp.zeros_like(value_sum)
    for number in range(heads):
        kv = number // groups
        at = slice(number * HEAD_DIM, (number + 1) * HEAD_DIM)
        key_at = (heads + kv) * HEAD_DIM
        value_at = (heads + key_heads + kv) * HEAD_DIM
        for first in range(0, length, QUERIES):
            rows = slice(first, first + QUERIES)
            keys = first + QUERIES
            slope = slopes[rows, at]
            delta = jnp.sum(slope.astype(F32) * mix_full[rows, at], axis=-1, keepdims=True)
            weight = probs[number, rows, :keys]
            weight_slope = nt(slope, rotated[:keys, value_at : value_at + HEAD_DIM])
            low = (weight.astype(F32) * (weight_slope - delta)).astype(BF)
            query = nn(low, rotated[:keys, key_at : key_at + HEAD_DIM]) * scale
            left, right = query[:, :HALF], query[:, HALF:]
            cos_here, sin_here = cosine[rows], sine[rows]
            lows[rows, at] = jnp.concatenate(
                [left * cos_here + right * sin_here, right * cos_here - left * sin_here], axis=1
            ).astype(BF)
            value_sum[kv, :, :keys] += tn(slope, weight)
            key_sum[kv, :, :keys] += tn(rotated[rows, at], low)
    for kv in range(key_heads):
        key = key_sum[kv].T * scale
        left, right = key[:, :HALF], key[:, HALF:]
        at = slice((heads + kv) * HEAD_DIM, (heads + kv + 1) * HEAD_DIM)
        lows[:, at] = jnp.concatenate(
            [left * cosine + right * sine, right * cosine - left * sine], axis=1
        ).astype(BF)
        at = slice((heads + key_heads + kv) * HEAD_DIM, (heads + key_heads + kv + 1) * HEAD_DIM)
        lows[:, at] = value_sum[kv].T.astype(BF)
    for number in range(seqs):
        lows_send[number] = lows[number * span : (number + 1) * span, :]
    grad = tn(attn_in[...], lows[...])
    part[:, :cols] = grad.astype(BF)
    gain_part = jnp.sum(grad * proj[...].astype(F32), axis=1, keepdims=True)
    lane = lax.broadcasted_iota(jnp.int32, (width, LANES), 1)
    part[:, cols:] = jnp.where(lane == 0, gain_part, 0.0).astype(BF)
    size = width // len(row_parts)
    for mask, row_part in enumerate(row_parts):
        spot = place[0] ^ mask
        row_part[...] = part[pl.ds(pl.multiple_of(spot * size, size), size), :]


def last_kernel(place, lows, half_one, half_two, small, own, resid_slope, hidden_grad, wide):
    put_pieces(place, wide, (half_one, half_two))
    joined = jnp.concatenate([lows[number] for number in range(lows.shape[0])], axis=1)
    slope = nt(joined, wide[...])
    block = own[...].astype(F32)
    inverse = lax.rsqrt(jnp.mean(block * block, axis=-1, keepdims=True) + EPS)
    scaled = slope * full_gain(small[...], 0)
    hidden_grad[...] = (
        resid_slope[...]
        + inverse * scaled
        - block * (inverse * inverse * inverse) * jnp.mean(scaled * block, axis=-1, keepdims=True)
    ).astype(BF)


def shards(
    hidden_in,
    segments,
    routes,
    cotangent,
    attn_gain,
    query_weight,
    key_weight,
    value_weight,
    out_weight,
    ffn_gain,
    router_weight,
    gate_weight,
    up_weight,
    down_weight,
):
    rows = lax.axis_size("row")
    far, near, cores = lax.axis_size("zh"), lax.axis_size("zl"), lax.axis_size("core")
    depth = far * near
    seqs = depth * cores
    span, width = hidden_in.shape[1:]
    length = span * seqs
    feats = query_weight.shape[0]
    experts = router_weight.shape[1]
    held, slab, hidden = gate_weight.shape
    mine = held // near
    team_size = rows * near
    tokens = team_size * span
    heads = HEADS // seqs
    groups = HEADS // KV_HEADS
    key_heads = max(1, heads // groups)
    query_cols, key_cols = heads * HEAD_DIM, key_heads * HEAD_DIM
    cols = query_cols + 2 * key_cols
    scale = HEAD_DIM**-0.5
    depth_place = lax.axis_index(DEPTH)
    near_place = lax.axis_index("zl")
    place = jnp.stack(
        [
            lax.axis_index("row"),
            depth_place,
            lax.axis_index("core"),
            lax.axis_index(ALL),
            near_place,
        ]
    ).astype(jnp.int32)
    own = hidden_in[0]

    starts = [(number * heads // groups) * HEAD_DIM for number in range(seqs)]
    room = -(-feats // TILE) * TILE
    packed, wide = run(
        functools.partial(pack_kernel, seqs, query_cols, key_cols, starts),
        "pack",
        (shape((seqs, room + TILE, cols), BF), shape((feats, seqs * cols), BF)),
        [SMEM] + [VMEM] * 7,
        (
            place,
            query_weight,
            key_weight,
            value_weight,
            router_weight.T,
            attn_gain[None],
            ffn_gain[None],
            segments,
        ),
        1,
    )
    line = [own, *(swap(own, DEPTH, mask) for mask in range(1, depth))]
    out_line = masked(out_weight.T, DEPTH)
    blocks = []
    for block in line:
        blocks += [block, swap(block, "core", 1)]
    packed = lax.all_to_all(packed, SEQ, 0, 0, tiled=True)
    packed, line[1] = tie(packed, line[1])
    packed = jnp.broadcast_to(packed, (rows, *packed.shape))
    packed = lax.all_to_all(packed, "row", 0, 0).reshape(rows * seqs, room + TILE, cols)
    proj = packed[:, :feats].reshape(width, cols)
    small = packed[:, room:]
    router_full = small[:, :, LANES : LANES + feats].transpose(1, 0, 2).reshape(experts, width)


    def row_blocks(block):
        return [block, *(swap(block, "row", mask) for mask in range(1, rows))]

    def near_blocks(block):
        return [block, *(swap(block, "zl", mask) for mask in range(1, near))]


    stacked = jnp.stack([gate_weight, up_weight, down_weight.transpose(0, 2, 1)])
    stacked = stacked.reshape(3, near, mine, slab, hidden)
    stacked = after(stacked, *line)

    def line_slabs(first, last):
        parts = []
        for mask in range(depth):
            part = lax.dynamic_index_in_dim(
                stacked[first:last], near_place ^ (mask % near), 1, False
            )
            parts.append(swap(part, DEPTH, mask) if mask else part)
        return parts

    gate_line = line_slabs(0, 1)
    up_near = near_blocks(cotangent[0])

    freq = THETA ** (-np.arange(HALF, dtype=np.float32) * 2.0 / HEAD_DIM)
    freq = jnp.asarray(freq, F32)[None]
    attn_in, rotated, turns, probs, mix_full, mix_send = run(
        functools.partial(attend_kernel, heads, key_heads, scale),
        "attend",
        (
            shape((length, width), BF),
            shape((length, cols), BF),
            shape((length, HEAD_DIM), F32),
            shape((heads, length, length), BF),
            shape((length, query_cols), F32),
            shape((seqs, span, query_cols), BF),
        ),
        [SMEM] + [VMEM] * (3 + len(blocks)),
        (place, freq, proj, small, *blocks),
        COST["attend"],
    )
    mix_send, gate_line, up_near, out_line = tie(mix_send, gate_line, up_near, out_line)
    out_rows = masked(jnp.stack(out_line), "row")
    gate_stack = jnp.stack(gate_line)
    gate_other = swap(gate_stack, "core", 1)
    upstream = row_blocks(jnp.stack(up_near))
    mix = lax.all_to_all(mix_send, SEQ, 0, 0, tiled=True)
    mix, gate_other, out_rows = tie(mix, gate_other, out_rows)
    out_halves = masked(jnp.stack(out_rows), "core")
    up_line = line_slabs(1, 2)

    residual, mix_low, ffn_in, gates, team_send, out_full = run(
        functools.partial(norm_kernel, experts),
        "norm",
        (
            shape((span, width), F32),
            shape((span, width), BF),
            shape((span, width), BF),
            shape((span, experts), F32),
            shape((span, width + LANES), BF),
            shape((width, width), BF),
        ),
        [SMEM] + [VMEM] * 7,
        (place, mix, own, small, router_full, routes[0], *out_halves),
        COST["norm"],
    )
    team = near_blocks(team_send)
    team = [row_blocks(block) for block in team]
    team[0], up_line, upstream = tie(team[0], up_line, upstream)
    up_stack = jnp.stack(up_line)
    up_other = swap(up_stack, "core", 1)
    down_line = line_slabs(2, 3)

    group_tokens = rows * span
    team_shape, up_shape = shape((group_tokens, width + LANES), BF), shape((group_tokens, width), BF)
    act_shape = shape((mine, group_tokens, hidden), BF)
    weight_scratch = pltpu.VMEM((mine, width, hidden), BF)

    def rise(low):
        return pl.pallas_call(
            functools.partial(rise_kernel, rows, low),
            out_shape=(team_shape, up_shape, act_shape, act_shape, act_shape),
            in_specs=[SMEM] + [ANY] * (2 * rows + 4),
            out_specs=(VMEM,) * 5,
            scratch_shapes=[
                weight_scratch,
                weight_scratch,
                pltpu.SemaphoreType.DMA((2 * rows + 2 * seqs,)),
            ],
            compiler_params=pltpu.CompilerParams(vmem_limit_bytes=VMEM_BYTES),
            cost_estimate=pl.CostEstimate(
                flops=int(COST["rise"] * 1e9), bytes_accessed=1024, transcendentals=0
            ),
            name="rise",
        )(place, *team[low], *upstream, gate_stack, gate_other, up_stack, up_other)

    def fall(risen):
        return pl.pallas_call(
            functools.partial(fall_kernel, rows, held, experts),
            out_shape=(
                *(shape((span, width + LANES), BF) for _ in range(rows)),
                shape((rows, span, width), BF),
                act_shape,
                act_shape,
            ),
            in_specs=[SMEM] + [VMEM] * 5 + [ANY] * 6,
            out_specs=(VMEM,) * (rows + 3),
            scratch_shapes=[
                pltpu.VMEM((group_tokens, width + LANES), BF),
                pltpu.VMEM((group_tokens, width), BF),
                weight_scratch,
                weight_scratch,
                weight_scratch,
                pltpu.SemaphoreType.DMA((3 * seqs,)),
            ],
            compiler_params=pltpu.CompilerParams(vmem_limit_bytes=VMEM_BYTES),
            cost_estimate=pl.CostEstimate(
                flops=int(COST["fall"] * 1e9), bytes_accessed=1024, transcendentals=0
            ),
            name="fall",
        )(place, *risen, gate_stack, gate_other, up_stack, up_other, down_stack, down_other)

    def joined(ours, theirs):
        kinds = ours.shape[1]
        parts = run(
            join_kernel,
            "join",
            tuple(shape((mine, slab, hidden), BF) for _ in range(kinds * depth)),
            [VMEM] * 2,
            (ours, theirs),
            COST["join"],
        )
        return [parts[kind * depth : (kind + 1) * depth] for kind in range(kinds)]

    def line_sends(parts):
        return [swap(part, DEPTH, mask) if mask else part for mask, part in enumerate(parts)]

    risen = []
    for low in range(near):
        results = rise(low)
        if low + 1 < near:
            results, team[low + 1] = tie(results, team[low + 1])
        risen.append(results)
    grad_scratch = [pltpu.VMEM((width, hidden), F32)]
    block = shape((depth, 1, mine, slab, hidden), BF)
    ours, theirs = run(
        functools.partial(down_kernel, near, held, experts),
        "down",
        (block, block),
        [SMEM] + [VMEM] * (3 * near),
        (place, *(value for part in risen for value in part[:3])),
        COST["down"],
        grad_scratch,
    )
    ours, theirs, down_line = tie(ours, theirs, down_line)
    down_stack = jnp.stack(down_line)
    down_other = swap(down_stack, "core", 1)
    theirs = swap(theirs, "core", 1)
    wide_line = masked(wide, DEPTH)

    def back_by_rows(group):
        return [swap(part, "row", mask) if mask else part for mask, part in enumerate(group)]

    slopes, outs, kept = [], [None] * near, []
    for low in reversed(range(near)):
        results = fall(risen[low])
        if low == near - 1:
            results, theirs, wide_line = tie(results, theirs, wide_line)
            wide_rows = masked(jnp.stack(wide_line), "row")
            down_sends = joined(ours, theirs)[0]
        else:
            results, part, wide_rows = tie(results, part, wide_rows)
            part = run(
                add_kernel,
                "add",
                shape((span, width + LANES), BF),
                [VMEM] * rows,
                tuple(part),
                COST["add"],
            )
            slopes.append(swap(part, "zl", low + 1))
        part = back_by_rows(results[:rows])
        outs[low] = results[rows]
        kept += [risen[low][0], *results[rows + 1 :]]
        if low == near - 1 and near > 1:
            risen[low - 1], down_sends = tie(risen[low - 1], down_sends)
    down_parts = line_sends(down_sends)
    slopes += part
    outs = jnp.concatenate(outs, axis=1)
    outs = lax.psum_scatter(outs, "row", scatter_dimension=0, tiled=True)[0]

    block = shape((depth, 2, mine, slab, hidden), BF)
    ours, theirs = run(
        functools.partial(weight_kernel, near),
        "weight",
        (block, block),
        [SMEM] + [VMEM] * (3 * near),
        (place, *kept),
        COST["weight"],
        grad_scratch,
    )
    ours, theirs, slopes, down_parts = tie(ours, theirs, slopes, down_parts)
    theirs = swap(theirs, "core", 1)

    resid_slope, mix_slope, out_part = run(
        back_kernel,
        "back",
        (
            shape((span, width), F32),
            shape((seqs, span, width // seqs), BF),
            shape((width, width + LANES), BF),
        ),
        [VMEM] * (8 + len(slopes)),
        (cotangent[0], residual, ffn_in, gates, router_full, small, out_full, mix_low, *slopes),
        COST["back"],
    )
    mix_slope, theirs = tie(mix_slope, theirs)
    mix_slope = lax.all_to_all(mix_slope, SEQ, 0, 0, tiled=True).reshape(length, query_cols)
    sends = joined(ours, theirs)
    mix_slope, sends = tie(mix_slope, sends)
    out_part = lax.psum_scatter(out_part, "row", scatter_dimension=0, tiled=True)
    parts = [line_sends(sends[0])]

    results = run(
        functools.partial(attend_back_kernel, heads, key_heads, scale),
        "attend_back",
        (
            shape((seqs, span, cols), BF),
            *(shape((width // rows, cols + LANES), BF) for _ in range(rows)),
        ),
        [SMEM] + [VMEM] * 7,
        (place, mix_slope, probs, rotated, mix_full, turns, attn_in, proj),
        COST["attend_back"],
        [
            pltpu.VMEM((length, cols), BF),
            pltpu.VMEM((key_heads, HEAD_DIM, length), F32),
            pltpu.VMEM((key_heads, HEAD_DIM, length), F32),
            pltpu.VMEM((width, cols + LANES), BF),
        ],
    )
    wide_halves = masked(jnp.stack(wide_rows), "core")
    results, parts, out_part, wide_halves = tie(results, parts, out_part, wide_halves)
    out_part = lax.psum_scatter(out_part, SEQ, scatter_dimension=0, tiled=True).astype(F32)
    lows_send = results[0]
    row_parts = back_by_rows(results[1:])
    lows = lax.all_to_all(lows_send, SEQ, 0, 0, tiled=True)
    lows, row_parts = tie(lows, row_parts)
    sends[1] = after(sends[1], lows)
    parts = [*parts[0], *line_sends(sends[1]), *down_parts]
    part = run(
        add_kernel,
        "add",
        shape((width // rows, cols + LANES), BF),
        [VMEM] * rows,
        tuple(row_parts),
        COST["add"],
    )
    hidden_grad = run(
        last_kernel,
        "last",
        shape((span, width), BF),
        [SMEM] + [VMEM] * 6,
        (place, lows, *wide_halves, small, own, resid_slope),
        COST["last"],
        [pltpu.VMEM((width, seqs * cols), BF)],
    )
    back = lax.all_to_all(part.reshape(seqs, feats, cols + LANES), SEQ, 0, 0, tiled=True)
    back = back.astype(F32)
    outs = after(outs, hidden_grad)
    outs = [
        swap(outs[low * span : (low + 1) * span], "zl", low) if low else outs[:span]
        for low in range(near)
    ]
    hidden_out = run(
        sum_kernel,
        "sum",
        shape((span, width), BF),
        [VMEM] * (1 + near),
        (residual, *outs),
        COST["sum"],
    )
    attn_gain_grad = jnp.sum(back[:, :, cols], axis=0) / attn_gain.astype(F32)
    query_grad = back[:, :, :query_cols].transpose(1, 0, 2).reshape(feats, HEADS * HEAD_DIM)

    def key_grads(share):
        times = seqs * key_heads // KV_HEADS
        share = share.reshape(seqs // times, times, feats, key_cols).sum(axis=1)
        return share.transpose(1, 0, 2).reshape(feats, KV_HEADS * HEAD_DIM)

    key_grad = key_grads(back[:, :, query_cols : query_cols + key_cols])
    value_grad = key_grads(back[:, :, query_cols + key_cols : cols])
    hidden_grad, hidden_out, parts = tie(hidden_grad, hidden_out, parts)
    gate_grad, up_grad, down_grad = run(
        functools.partial(share_kernel, near),
        "share",
        (
            shape((held, slab, hidden), F32),
            shape((held, slab, hidden), F32),
            shape((held, hidden, slab), F32),
        ),
        [SMEM] + [VMEM] * (3 * depth),
        (place, *parts),
        COST["share"],
    )
    return (
        hidden_out[None],
        hidden_grad[None],
        attn_gain_grad,
        query_grad,
        key_grad,
        value_grad,
        out_part[:, :width].T,
        out_part[:, width + experts],
        out_part[:, width : width + experts],
        gate_grad,
        up_grad,
        down_grad,
    )


COST = {
    "attend": 12,
    "norm": 4,
    "rise": 6,
    "down": 5,
    "fall": 10,
    "weight": 9,
    "join": 3,
    "back": 5,
    "attend_back": 11,
    "last": 4,
    "sum": 2,
    "add": 1,
    "share": 3,
}


def solution(mesh):
    rows, seqs = mesh.shape["row"], mesh.shape["seq"]
    depth = seqs // 2
    held = 16 // rows
    near = min(GROUP, held, depth)
    fine = Mesh(mesh.devices.reshape(rows, depth // near, near, 2), ALL)
    token = P("row", SEQ, None)
    flat, dense = P(ALL), P(ALL, None)
    specs_in = (token, P("row", SEQ), token, token, flat, dense, dense, dense, P(None, ALL), flat, dense)
    specs_out = (token, token, flat, dense, dense, dense, P(None, ALL), flat, dense)
    owned = (token, token, P("row", None, SEQ))
    return jax.shard_map(
        shards,
        mesh=fine,
        in_specs=specs_in + owned,
        out_specs=specs_out + owned,
        check_vma=False,
    )
```

```python
import functools

import jax
import jax.numpy as jnp
import numpy as np
from jax import lax
from jax.experimental import pallas as pl
from jax.experimental.pallas import tpu as pltpu
from jax.sharding import Mesh
from jax.sharding import PartitionSpec as P

HEADS = 16
KV_HEADS = 8
HEAD_DIM = 64
HALF = HEAD_DIM // 2

EPS = 1e-06
THETA = 10000.0
NEG = -1e30
GROUP = 2
LANES = 128
TILE = 16
COUNTS = 160
QUERIES = 256
CHUNK = 256
VMEM_BYTES = 34 * 1024 * 1024

BF = jnp.bfloat16
F32 = jnp.float32

SEQ = ("zh", "zl", "core")
DEPTH = ("zh", "zl")
ALL = ("row", "zh", "zl", "core")
TEAM = ("row", "zl")

SMEM = pl.BlockSpec(memory_space=pltpu.SMEM)
VMEM = pl.BlockSpec(memory_space=pltpu.VMEM)
ANY = pl.BlockSpec(memory_space=pl.ANY)


def nt(left, right):
    return lax.dot_general(left, right, (((1,), (1,)), ((), ())), preferred_element_type=F32)


def nn(left, right):
    return lax.dot_general(left, right, (((1,), (0,)), ((), ())), preferred_element_type=F32)


def tn(left, right):
    return lax.dot_general(left, right, (((0,), (0,)), ((), ())), preferred_element_type=F32)


def shape(dims, kind):
    return jax.ShapeDtypeStruct(dims, kind)


def run(kernel, name, out_shape, in_specs, args, micros, scratch=()):
    return pl.pallas_call(
        kernel,
        out_shape=out_shape,
        in_specs=in_specs,
        out_specs=jax.tree.map(lambda _: VMEM, out_shape),
        scratch_shapes=list(scratch),
        compiler_params=pltpu.CompilerParams(vmem_limit_bytes=VMEM_BYTES),
        cost_estimate=pl.CostEstimate(
            flops=int(micros * 1e9), bytes_accessed=1024, transcendentals=0
        ),
        name=name,
    )(*args)


def after(value, *earlier):
    return lax.optimization_barrier((value, *earlier))[0]


def tie(*values):
    return lax.optimization_barrier(values)


def swap(block, axes, mask):
    return lax.ppermute(block, axes, [(i, i ^ mask) for i in range(lax.axis_size(axes))])


def masked(block, axes):
    return [swap(block, axes, mask) if mask else block for mask in range(lax.axis_size(axes))]


def pack_kernel(seqs, query_cols, key_cols, starts, place, query, key, value, router, gain_one, gain_two, segs, out, wide):
    feats = query.shape[0]
    room = out.shape[1] - TILE
    cols = out.shape[2]
    mine = place[3]
    row = lax.broadcasted_iota(jnp.int32, (TILE, LANES), 0)
    lane = lax.broadcasted_iota(jnp.int32, (TILE, LANES), 1)
    times = LANES // feats
    one = jnp.concatenate([gain_one[...].astype(F32)] * times, axis=1)
    two = jnp.concatenate([gain_two[...].astype(F32)] * times, axis=1)
    slot = (row % 8) * times + lane // feats
    gains = jnp.where(slot == mine, jnp.where(row < 8, one, two), 0.0)
    ids = segs[...]
    below_one = jnp.sum((ids < 1).astype(F32), axis=1, keepdims=True)
    below_two = jnp.sum((ids < 2).astype(F32), axis=1, keepdims=True)
    side = lax.broadcasted_iota(jnp.int32, (TILE, HALF), 0)
    counts = jnp.where(side == 0, below_one, jnp.where(side == 1, below_two, 0.0))
    small = [gains, router[...].astype(F32)]
    if feats < HALF:
        small.append(jnp.zeros((TILE, HALF - feats), F32))
    small.append(counts)
    if cols > COUNTS + HALF:
        small.append(jnp.zeros((TILE, cols - COUNTS - HALF), F32))
    small = jnp.concatenate(small, axis=1).astype(BF)
    for number in range(seqs):
        first = starts[number]
        block = jnp.concatenate(
            [
                query[:, number * query_cols : (number + 1) * query_cols].astype(F32),
                key[:, first : first + key_cols].astype(F32),
                value[:, first : first + key_cols].astype(F32),
            ],
            axis=1,
        )
        wide[:, number * cols : (number + 1) * cols] = block.astype(BF)
        if room > feats:
            block = jnp.concatenate([block, jnp.zeros((room - feats, cols), F32)], axis=0)
        out[number, :room] = block.astype(BF)
        out[number, room:] = small


def full_gain(small, first):
    total = jnp.sum(small[:, first : first + 8, :LANES].astype(F32), axis=0)
    return jnp.concatenate([total[i : i + 1] for i in range(8)], axis=1)


def attend_kernel(heads, key_heads, scale, place, freq, proj, small, *refs):
    parts = refs[:-6]
    attn_in, rotated, turns, probs, mix_full, mix_send = refs[-6:]
    span = parts[0].shape[0]
    length = attn_in.shape[0]
    seqs = len(parts)
    gain = full_gain(small[...], 0)
    for number, part in enumerate(parts):
        mask, core = number // 2, number % 2
        spot = (place[1] ^ mask) * 2 + (place[2] ^ core)
        block = part[...].astype(F32)
        inverse = lax.rsqrt(jnp.mean(block * block, axis=-1, keepdims=True) + EPS)
        attn_in[pl.ds(pl.multiple_of(spot * span, span), span), :] = (block * inverse * gain).astype(BF)
    counts = jnp.sum(small[pl.ds(place[0] * seqs, seqs)].astype(F32), axis=0)
    below_one = counts[0:1, COUNTS : COUNTS + 1].astype(jnp.int32)
    below_two = counts[1:2, COUNTS : COUNTS + 1].astype(jnp.int32)
    index = lax.broadcasted_iota(jnp.int32, (length, 1), 0)
    start = jnp.where(index >= below_two, below_two, jnp.where(index >= below_one, below_one, 0))
    angles = (index - start).astype(F32) * freq[...]
    cosine, sine = jnp.cos(angles), jnp.sin(angles)
    turns[...] = jnp.concatenate([cosine, sine], axis=1)
    pre = nn(attn_in[...], proj[...])

    def turned(number):
        first = pre[:, number * HEAD_DIM : number * HEAD_DIM + HALF]
        second = pre[:, number * HEAD_DIM + HALF : (number + 1) * HEAD_DIM]
        return [first * cosine - second * sine, second * cosine + first * sine]

    pieces = []
    for number in range(heads + key_heads):
        pieces += turned(number)
    pieces.append(pre[:, (heads + key_heads) * HEAD_DIM :])
    rotated[...] = jnp.concatenate(pieces, axis=1).astype(BF)
    groups = heads // key_heads
    for number in range(heads):
        kv = number // groups
        key_at = (heads + kv) * HEAD_DIM
        value_at = (heads + key_heads + kv) * HEAD_DIM
        for first in range(0, length, QUERIES):
            rows = slice(first, first + QUERIES)
            keys = first + QUERIES
            query = rotated[rows, number * HEAD_DIM : (number + 1) * HEAD_DIM]
            scores = nt(query, rotated[:keys, key_at : key_at + HEAD_DIM]) * scale
            column = lax.broadcasted_iota(jnp.int32, (QUERIES, keys), 1)
            allowed = (column <= index[rows]) & (column >= start[rows])
            scores = jnp.where(allowed, scores, NEG)
            raised = jnp.exp(scores - jnp.max(scores, axis=-1, keepdims=True))
            weight = (raised / jnp.sum(raised, axis=-1, keepdims=True)).astype(BF)
            probs[number, rows, :keys] = weight
            mix = nn(weight, rotated[:keys, value_at : value_at + HEAD_DIM])
            mix_full[rows, number * HEAD_DIM : (number + 1) * HEAD_DIM] = mix
    for number in range(seqs):
        mix_send[number] = mix_full[number * span : (number + 1) * span].astype(BF)


def put_pieces(place, target, halves):
    for core, half in enumerate(halves):
        for mask in range(half.shape[0]):
            for deep in range(half.shape[1]):
                spot = ((place[0] ^ mask) * half.shape[1] + (place[1] ^ deep)) * 2 + (place[2] ^ core)
                folds = target.shape[1] // half.shape[3]
                feats = half.shape[2] // folds
                rows = pl.ds(pl.multiple_of(spot * feats, feats), feats)
                for fold in range(folds):
                    columns = slice(fold * half.shape[3], (fold + 1) * half.shape[3])
                    target[rows, columns] = half[mask, deep, fold * feats : (fold + 1) * feats]


def norm_kernel(experts, place, mix, own, small, router, routes, half_one, half_two, residual, mix_low, ffn_in, gates, send, out_full):
    span, width = own.shape
    put_pieces(place, out_full, (half_one, half_two))
    mix_low[...] = jnp.concatenate([mix[number] for number in range(mix.shape[0])], axis=1)
    total = own[...].astype(F32) + nt(mix_low[...], out_full[...])
    residual[...] = total
    inverse = lax.rsqrt(jnp.mean(total * total, axis=-1, keepdims=True) + EPS)
    normed = (total * inverse * full_gain(small[...], 8)).astype(BF)
    ffn_in[...] = normed
    logits = nt(normed, router[...])
    number = lax.broadcasted_iota(jnp.int32, (span, experts), 1)
    named = number < 0
    for choice in range(routes.shape[1]):
        named = named | (routes[:, choice : choice + 1] == number)
    logits = jnp.where(named, logits, NEG)
    raised = jnp.where(named, jnp.exp(logits - jnp.max(logits, axis=-1, keepdims=True)), 0.0)
    shares = raised / jnp.sum(raised, axis=-1, keepdims=True)
    gates[...] = shares
    high = shares.astype(BF).astype(F32)
    extra = jnp.concatenate(
        [high, shares - high, jnp.zeros((span, LANES - 2 * experts), F32)], axis=1
    ).astype(BF)
    send[:, :width] = normed
    send[:, width:] = extra


def expert_gate(team, rows, width, experts, expert):
    lane = (lax.broadcasted_iota(jnp.int32, (1, experts), 1) == expert).astype(F32)
    extra = team[rows, width : width + LANES].astype(F32)
    gate = (extra[:, :experts] + extra[:, experts : 2 * experts]) * lane
    return jnp.sum(gate, axis=1, keepdims=True)


def gather_slabs(place, pairs, targets, begin):
    kinds = [(pair, kind) for pair in pairs for kind in range(pair[0].shape[1])]
    for (pair, kind), target in zip(kinds, targets):
        depth, _, _, slab, _ = pair[0].shape
        for core, part in enumerate(pair):
            for mask in range(depth):
                spot = (place[1] ^ mask) * 2 + (place[2] ^ core)
                rows = pl.ds(pl.multiple_of(spot * slab, slab), slab)
                begin(part.at[mask, kind], target.at[:, rows, :])


def copier(sems):
    copies = []

    def begin(source, target):
        copy = pltpu.make_async_copy(source, target, sems.at[len(copies)])
        copy.start()
        copies.append(copy)

    return copies, begin


def rise_kernel(count, low, place, *refs):
    team_parts, up_parts, slabs = refs[:count], refs[count : 2 * count], refs[2 * count : 2 * count + 4]
    team, upstream, act, gate_pres, up_pres, gate_w, up_w, sems = refs[2 * count + 4 :]
    span, width = up_parts[0].shape[1:]
    mine = act.shape[0]
    copies, begin = copier(sems)
    for number in range(count):
        rows = pl.ds(number * span, span)
        begin(team_parts[number], team.at[rows, :])
        begin(up_parts[number].at[low], upstream.at[rows, :])
    gather_slabs(place, (slabs[:2], slabs[2:]), (gate_w, up_w), begin)
    for copy in copies:
        copy.wait()

    def step(number, carry):
        rows = pl.ds(pl.multiple_of(number * CHUNK, CHUNK), CHUNK)
        inputs = team[rows, :width]
        for place_here in range(mine):
            gate_pre = nn(inputs, gate_w[place_here])
            up_pre = nn(inputs, up_w[place_here])
            sigmoid = 1.0 / (1.0 + jnp.exp(-gate_pre))
            act[place_here, rows, :] = (gate_pre * sigmoid * up_pre).astype(BF)
            gate_pres[place_here, rows, :] = gate_pre.astype(BF)
            up_pres[place_here, rows, :] = up_pre.astype(BF)
        return carry

    lax.fori_loop(0, count * span // CHUNK, step, 0)


def fall_kernel(count, held, experts, place, team, upstream, act, gate_pres, up_pres, *refs):
    slabs, slope_parts, out, refs = refs[:6], refs[6 : 6 + count], refs[6 + count], refs[7 + count :]
    gate_low, up_low, slopes, outs, gate_w, up_w, down_w, sems = refs
    tokens, width = upstream.shape
    span = tokens // count
    mine = act.shape[0]
    copies, begin = copier(sems)
    gather_slabs(place, (slabs[:2], slabs[2:4], slabs[4:]), (gate_w, up_w, down_w), begin)
    for copy in copies:
        copy.wait()

    def step(number, carry):
        rows = pl.ds(pl.multiple_of(number * CHUNK, CHUNK), CHUNK)
        up_f = upstream[rows, :].astype(F32)
        out_sum = jnp.zeros((CHUNK, width), F32)
        slope_sum = jnp.zeros((CHUNK, width), F32)
        columns = jnp.zeros((CHUNK, LANES), F32)
        for place_here in range(mine):
            expert = place[0] * held + place[4] * mine + place_here
            gate = expert_gate(team, rows, width, experts, expert)
            expert_out = nt(act[place_here, rows, :], down_w[place_here])
            out_sum = out_sum + gate * expert_out
            score = jnp.sum(up_f * expert_out, axis=1, keepdims=True)
            lane = lax.broadcasted_iota(jnp.int32, (1, LANES), 1)
            columns = jnp.where(lane == expert, score, columns)
            hidden_slope = nn((gate * up_f).astype(BF), down_w[place_here])
            gate_pre = gate_pres[place_here, rows, :].astype(F32)
            up_pre = up_pres[place_here, rows, :].astype(F32)
            sigmoid = 1.0 / (1.0 + jnp.exp(-gate_pre))
            gate_slope = hidden_slope * up_pre * sigmoid * (1.0 + gate_pre * (1.0 - sigmoid))
            gate_slope = gate_slope.astype(BF)
            up_slope = (hidden_slope * gate_pre * sigmoid).astype(BF)
            gate_low[place_here, rows, :] = gate_slope
            up_low[place_here, rows, :] = up_slope
            slope_sum = slope_sum + nt(gate_slope, gate_w[place_here])
            slope_sum = slope_sum + nt(up_slope, up_w[place_here])
        slopes[rows, :width] = slope_sum.astype(BF)
        slopes[rows, width:] = columns.astype(BF)
        outs[rows, :] = out_sum.astype(BF)
        return carry

    lax.fori_loop(0, tokens // CHUNK, step, 0)
    for number in range(count):
        rows = slice(number * span, (number + 1) * span)
        slope_parts[number][...] = slopes[rows, :]
        out[number] = outs[rows, :]


def spread_grad(place, total, kind, number, ours, theirs):
    slab = ours.shape[3]
    for mask in range(ours.shape[0]):
        for core, target in ((0, ours), (1, theirs)):
            spot = (place[1] ^ mask) * 2 + (place[2] ^ core)
            block = total[pl.ds(pl.multiple_of(spot * slab, slab), slab), :]
            target[mask, kind, number] = block.astype(BF)


def down_kernel(halves, held, experts, place, *refs):
    groups = [refs[3 * number : 3 * number + 3] for number in range(halves)]
    ours, theirs, total = refs[3 * halves :]
    mine = groups[0][2].shape[0]
    width = groups[0][1].shape[1]
    for place_here in range(mine):
        expert = place[0] * held + place[4] * mine + place_here
        for number, (team, upstream, act) in enumerate(groups):
            gate = expert_gate(team, slice(None), width, experts, expert)
            grad = tn((gate * upstream[...].astype(F32)).astype(BF), act[place_here])
            if number == 0:
                total[...] = grad
            else:
                total[...] += grad
        spread_grad(place, total, 0, place_here, ours, theirs)


def weight_kernel(halves, place, *refs):
    groups = [refs[3 * number : 3 * number + 3] for number in range(halves)]
    ours, theirs, total = refs[3 * halves :]
    mine = groups[0][1].shape[0]
    width = total.shape[0]
    for kind in range(2):
        for place_here in range(mine):
            for number, (team, *lows) in enumerate(groups):
                grad = tn(team[:, :width], lows[kind][place_here])
                if number == 0:
                    total[...] = grad
                else:
                    total[...] += grad
            spread_grad(place, total, kind, place_here, ours, theirs)


def join_kernel(ours, others, *outs):
    depth = ours.shape[0]
    for number, out in enumerate(outs):
        kind, mask = number // depth, number % depth
        out[...] = (ours[mask, kind].astype(F32) + others[mask, kind].astype(F32)).astype(BF)


def share_kernel(near, place, *refs):
    parts, outs = refs[:-3], refs[-3:]
    depth = len(parts) // 3
    mine = parts[0].shape[0]
    for low in range(near):
        owner = place[4] ^ low
        for number in range(mine):
            for kind, out in enumerate(outs):
                of_kind = parts[kind * depth : (kind + 1) * depth]
                total = sum(part[number].astype(F32) for part in of_kind[low::near])
                out[owner * mine + number] = total if kind < 2 else total.T


def stack_kernel(*refs):
    for number, part in enumerate(refs[:-1]):
        refs[-1][number] = part[...]


def add_kernel(*refs):
    total = refs[0][...].astype(F32)
    for part in refs[1:-1]:
        total = total + part[...].astype(F32)
    refs[-1][...] = total.astype(BF)


def sum_kernel(residual, *refs):
    total = residual[...]
    width = total.shape[1]
    for part in refs[:-1]:
        total = total + part[:, part.shape[1] - width :].astype(F32)
    refs[-1][...] = total.astype(BF)


def back_kernel(cotangent, residual, ffn_in, gates, router, small, out_full, mix_low, *refs):
    slopes, (resid_slope, mix_send, out_part) = refs[:-3], refs[-3:]
    span, width = residual.shape
    experts = gates.shape[1]
    back = slopes[0][:, : width + LANES].astype(F32)
    for part in slopes[1:]:
        back = back + part[:, : width + LANES].astype(F32)
    scores = back[:, width : width + experts]
    shares = gates[...]
    logit_slope = shares * (scores - jnp.sum(shares * scores, axis=-1, keepdims=True))
    logit_slope = logit_slope.astype(BF)
    total = residual[...]
    inverse = lax.rsqrt(jnp.mean(total * total, axis=-1, keepdims=True) + EPS)
    ffn_slope = back[:, :width] + nn(logit_slope, router[...])
    scaled = ffn_slope * full_gain(small[...], 8)
    slope = (
        cotangent[...].astype(F32)
        + inverse * scaled
        - total * (inverse * inverse * inverse) * jnp.mean(scaled * total, axis=-1, keepdims=True)
    )
    resid_slope[...] = slope
    low = slope.astype(BF)
    mix_slope = nn(low, out_full[...]).astype(BF)
    cols = width // mix_send.shape[0]
    for number in range(mix_send.shape[0]):
        mix_send[number] = mix_slope[:, number * cols : (number + 1) * cols]
    out_part[:, :width] = tn(low, mix_low[...]).astype(BF)
    router_part = tn(ffn_in[...], logit_slope)
    gain_part = jnp.sum((ffn_slope * total * inverse).T, axis=1, keepdims=True)
    out_part[:, width:] = jnp.concatenate(
        [router_part, gain_part, jnp.zeros((width, LANES - experts - 1), F32)], axis=1
    ).astype(BF)


def attend_back_kernel(heads, key_heads, scale, place, slopes, probs, rotated, mix_full, turns, attn_in, proj, lows_send, *refs):
    row_parts, (lows, key_sum, value_sum, part) = refs[:-4], refs[-4:]
    length, width = attn_in.shape
    seqs, span, cols = lows_send.shape
    cosine, sine = turns[:, :HALF], turns[:, HALF:]
    groups = heads // key_heads
    key_sum[...] = jnp.zeros_like(key_sum)
    value_sum[...] = jnp.zeros_like(value_sum)
    for number in range(heads):
        kv = number // groups
        at = slice(number * HEAD_DIM, (number + 1) * HEAD_DIM)
        key_at = (heads + kv) * HEAD_DIM
        value_at = (heads + key_heads + kv) * HEAD_DIM
        for first in range(0, length, QUERIES):
            rows = slice(first, first + QUERIES)
            keys = first + QUERIES
            slope = slopes[rows, at]
            delta = jnp.sum(slope.astype(F32) * mix_full[rows, at], axis=-1, keepdims=True)
            weight = probs[number, rows, :keys]
            weight_slope = nt(slope, rotated[:keys, value_at : value_at + HEAD_DIM])
            low = (weight.astype(F32) * (weight_slope - delta)).astype(BF)
            query = nn(low, rotated[:keys, key_at : key_at + HEAD_DIM]) * scale
            left, right = query[:, :HALF], query[:, HALF:]
            cos_here, sin_here = cosine[rows], sine[rows]
            lows[rows, at] = jnp.concatenate(
                [left * cos_here + right * sin_here, right * cos_here - left * sin_here], axis=1
            ).astype(BF)
            value_sum[kv, :, :keys] += tn(slope, weight)
            key_sum[kv, :, :keys] += tn(rotated[rows, at], low)
    for kv in range(key_heads):
        key = key_sum[kv].T * scale
        left, right = key[:, :HALF], key[:, HALF:]
        at = slice((heads + kv) * HEAD_DIM, (heads + kv + 1) * HEAD_DIM)
        lows[:, at] = jnp.concatenate(
            [left * cosine + right * sine, right * cosine - left * sine], axis=1
        ).astype(BF)
        at = slice((heads + key_heads + kv) * HEAD_DIM, (heads + key_heads + kv + 1) * HEAD_DIM)
        lows[:, at] = value_sum[kv].T.astype(BF)
    for number in range(seqs):
        lows_send[number] = lows[number * span : (number + 1) * span, :]
    grad = tn(attn_in[...], lows[...])
    part[:, :cols] = grad.astype(BF)
    gain_part = jnp.sum(grad * proj[...].astype(F32), axis=1, keepdims=True)
    lane = lax.broadcasted_iota(jnp.int32, (width, LANES), 1)
    part[:, cols:] = jnp.where(lane == 0, gain_part, 0.0).astype(BF)
    size = width // len(row_parts)
    for mask, row_part in enumerate(row_parts):
        spot = place[0] ^ mask
        row_part[...] = part[pl.ds(pl.multiple_of(spot * size, size), size), :]


def last_kernel(place, lows, half_one, half_two, small, own, resid_slope, hidden_grad, wide):
    put_pieces(place, wide, (half_one, half_two))
    joined = jnp.concatenate([lows[number] for number in range(lows.shape[0])], axis=1)
    slope = nt(joined, wide[...])
    block = own[...].astype(F32)
    inverse = lax.rsqrt(jnp.mean(block * block, axis=-1, keepdims=True) + EPS)
    scaled = slope * full_gain(small[...], 0)
    hidden_grad[...] = (
        resid_slope[...]
        + inverse * scaled
        - block * (inverse * inverse * inverse) * jnp.mean(scaled * block, axis=-1, keepdims=True)
    ).astype(BF)


def shards(
    hidden_in,
    segments,
    routes,
    cotangent,
    attn_gain,
    query_weight,
    key_weight,
    value_weight,
    out_weight,
    ffn_gain,
    router_weight,
    gate_weight,
    up_weight,
    down_weight,
):
    rows = lax.axis_size("row")
    far, near, cores = lax.axis_size("zh"), lax.axis_size("zl"), lax.axis_size("core")
    depth = far * near
    seqs = depth * cores
    span, width = hidden_in.shape[1:]
    length = span * seqs
    feats = query_weight.shape[0]
    experts = router_weight.shape[1]
    held, slab, hidden = gate_weight.shape
    mine = held // near
    team_size = rows * near
    tokens = team_size * span
    heads = HEADS // seqs
    groups = HEADS // KV_HEADS
    key_heads = max(1, heads // groups)
    query_cols, key_cols = heads * HEAD_DIM, key_heads * HEAD_DIM
    cols = query_cols + 2 * key_cols
    scale = HEAD_DIM**-0.5
    depth_place = lax.axis_index(DEPTH)
    near_place = lax.axis_index("zl")
    place = jnp.stack(
        [
            lax.axis_index("row"),
            depth_place,
            lax.axis_index("core"),
            lax.axis_index(ALL),
            near_place,
        ]
    ).astype(jnp.int32)
    own = hidden_in[0]

    starts = [(number * heads // groups) * HEAD_DIM for number in range(seqs)]
    room = -(-feats // TILE) * TILE
    packed, wide = run(
        functools.partial(pack_kernel, seqs, query_cols, key_cols, starts),
        "pack",
        (shape((seqs, room + TILE, cols), BF), shape((feats, seqs * cols), BF)),
        [SMEM] + [VMEM] * 7,
        (
            place,
            query_weight,
            key_weight,
            value_weight,
            router_weight.T,
            attn_gain[None],
            ffn_gain[None],
            segments,
        ),
        1,
    )
    line = [own, *(swap(own, DEPTH, mask) for mask in range(1, depth))]
    blocks = []
    for block in line:
        blocks += [block, swap(block, "core", 1)]
    packed = lax.all_to_all(packed, SEQ, 0, 0, tiled=True)
    packed, line[1] = tie(packed, line[1])
    packed = jnp.broadcast_to(packed, (rows, *packed.shape))
    packed = lax.all_to_all(packed, "row", 0, 0).reshape(rows * seqs, room + TILE, cols)
    packed, up_near = tie(packed, masked(cotangent[0], "zl"))
    upstream = masked(jnp.stack(up_near), "row")
    proj = packed[:, :feats].reshape(width, cols)
    small = packed[:, room:]
    router_full = small[:, :, LANES : LANES + feats].transpose(1, 0, 2).reshape(experts, width)


    def row_blocks(block):
        return [block, *(swap(block, "row", mask) for mask in range(1, rows))]

    def near_blocks(block):
        return [block, *(swap(block, "zl", mask) for mask in range(1, near))]


    stacked = jnp.stack([gate_weight, up_weight, down_weight.transpose(0, 2, 1)])
    stacked = stacked.reshape(3, near, mine, slab, hidden)
    stacked = after(stacked, *line)

    def line_slabs(first, last):
        parts = []
        for mask in range(depth):
            part = lax.dynamic_index_in_dim(
                stacked[first:last], near_place ^ (mask % near), 1, False
            )
            parts.append(swap(part, DEPTH, mask) if mask else part)
        return parts

    folded = jnp.concatenate(jnp.split(out_weight.T, width // hidden, axis=1), axis=0)
    size = mine * slab
    gate_line = []
    for mask in range(depth):
        part = lax.dynamic_index_in_dim(stacked[0], near_place ^ (mask % near), 0, False)
        part = jnp.concatenate([part.reshape(size, hidden), folded], axis=0)
        gate_line.append(swap(part, DEPTH, mask) if mask else part)

    freq = THETA ** (-np.arange(HALF, dtype=np.float32) * 2.0 / HEAD_DIM)
    freq = jnp.asarray(freq, F32)[None]
    attn_in, rotated, turns, probs, mix_full, mix_send = run(
        functools.partial(attend_kernel, heads, key_heads, scale),
        "attend",
        (
            shape((length, width), BF),
            shape((length, cols), BF),
            shape((length, HEAD_DIM), F32),
            shape((heads, length, length), BF),
            shape((length, query_cols), F32),
            shape((seqs, span, query_cols), BF),
        ),
        [SMEM] + [VMEM] * (3 + len(blocks)),
        (place, freq, proj, small, *blocks),
        COST["attend"],
    )
    mix_send, gate_line, upstream = tie(mix_send, gate_line, upstream)
    out_line = [part[size:] for part in gate_line]
    gate_line = [part[:size].reshape(1, mine, slab, hidden) for part in gate_line]
    out_rows = masked(jnp.stack(out_line), "row")
    gate_stack = jnp.stack(gate_line)
    gate_other = swap(gate_stack, "core", 1)
    mix = lax.all_to_all(mix_send, SEQ, 0, 0, tiled=True)
    mix, gate_other, out_rows = tie(mix, gate_other, out_rows)
    out_halves = masked(jnp.stack(out_rows), "core")
    up_line = line_slabs(1, 2)

    residual, mix_low, ffn_in, gates, team_send, out_full = run(
        functools.partial(norm_kernel, experts),
        "norm",
        (
            shape((span, width), F32),
            shape((span, width), BF),
            shape((span, width), BF),
            shape((span, experts), F32),
            shape((span, width + LANES), BF),
            shape((width, width), BF),
        ),
        [SMEM] + [VMEM] * 7,
        (place, mix, own, small, router_full, routes[0], *out_halves),
        COST["norm"],
    )
    team = near_blocks(team_send)
    team = [row_blocks(block) for block in team]
    wide_line = masked(wide, DEPTH)
    team[0], wide_line = tie(team[0], wide_line)
    wide_rows = masked(jnp.stack(wide_line), "row")
    up_stack = run(
        stack_kernel,
        "stack",
        shape((depth, 1, mine, slab, hidden), BF),
        [VMEM] * depth,
        tuple(up_line),
        COST["stack"],
    )
    up_other = swap(up_stack, "core", 1)
    down_line = line_slabs(2, 3)

    group_tokens = rows * span
    team_shape, up_shape = shape((group_tokens, width + LANES), BF), shape((group_tokens, width), BF)
    act_shape = shape((mine, group_tokens, hidden), BF)
    weight_scratch = pltpu.VMEM((mine, width, hidden), BF)

    def rise(low):
        return pl.pallas_call(
            functools.partial(rise_kernel, rows, low),
            out_shape=(team_shape, up_shape, act_shape, act_shape, act_shape),
            in_specs=[SMEM] + [ANY] * (2 * rows + 4),
            out_specs=(VMEM,) * 5,
            scratch_shapes=[
                weight_scratch,
                weight_scratch,
                pltpu.SemaphoreType.DMA((2 * rows + 2 * seqs,)),
            ],
            compiler_params=pltpu.CompilerParams(vmem_limit_bytes=VMEM_BYTES),
            cost_estimate=pl.CostEstimate(
                flops=int(COST["rise"] * 1e9), bytes_accessed=1024, transcendentals=0
            ),
            name="rise",
        )(place, *team[low], *upstream, gate_stack, gate_other, up_stack, up_other)

    def fall(risen):
        return pl.pallas_call(
            functools.partial(fall_kernel, rows, held, experts),
            out_shape=(
                *(shape((span, width + LANES), BF) for _ in range(rows)),
                shape((rows, span, width), BF),
                act_shape,
                act_shape,
            ),
            in_specs=[SMEM] + [VMEM] * 5 + [ANY] * 6,
            out_specs=(VMEM,) * (rows + 3),
            scratch_shapes=[
                pltpu.VMEM((group_tokens, width + LANES), BF),
                pltpu.VMEM((group_tokens, width), BF),
                weight_scratch,
                weight_scratch,
                weight_scratch,
                pltpu.SemaphoreType.DMA((3 * seqs,)),
            ],
            compiler_params=pltpu.CompilerParams(vmem_limit_bytes=VMEM_BYTES),
            cost_estimate=pl.CostEstimate(
                flops=int(COST["fall"] * 1e9), bytes_accessed=1024, transcendentals=0
            ),
            name="fall",
        )(place, *risen, gate_stack, gate_other, up_stack, up_other, down_stack, down_other)

    def joined(ours, theirs):
        kinds = ours.shape[1]
        parts = run(
            join_kernel,
            "join",
            tuple(shape((mine, slab, hidden), BF) for _ in range(kinds * depth)),
            [VMEM] * 2,
            (ours, theirs),
            COST["join"],
        )
        return [parts[kind * depth : (kind + 1) * depth] for kind in range(kinds)]

    def line_sends(parts):
        return [swap(part, DEPTH, mask) if mask else part for mask, part in enumerate(parts)]

    risen = []
    for low in range(near):
        results = rise(low)
        if low + 1 < near:
            results, team[low + 1] = tie(results, team[low + 1])
        risen.append(results)
    grad_scratch = [pltpu.VMEM((width, hidden), F32)]
    block = shape((depth, 1, mine, slab, hidden), BF)
    ours, theirs = run(
        functools.partial(down_kernel, near, held, experts),
        "down",
        (block, block),
        [SMEM] + [VMEM] * (3 * near),
        (place, *(value for part in risen for value in part[:3])),
        COST["down"],
        grad_scratch,
    )
    ours, theirs, down_line, wide_rows = tie(ours, theirs, down_line, wide_rows)
    wide_halves = masked(jnp.stack(wide_rows), "core")
    down_stack = jnp.stack(down_line)
    down_other = swap(down_stack, "core", 1)
    theirs = swap(theirs, "core", 1)

    def back_by_rows(group):
        return [swap(part, "row", mask) if mask else part for mask, part in enumerate(group)]

    slopes, outs, kept = [], [None] * near, []
    for low in reversed(range(near)):
        results = fall(risen[low])
        if low == near - 1:
            results, theirs, wide_halves = tie(results, theirs, wide_halves)
            down_sends = joined(ours, theirs)[0]
        else:
            results, part = tie(results, part)
            part = run(
                add_kernel,
                "add",
                shape((span, width + LANES), BF),
                [VMEM] * rows,
                tuple(part),
                COST["add"],
            )
            slopes.append(swap(part, "zl", low + 1))
        part = back_by_rows(results[:rows])
        outs[low] = results[rows]
        kept += [risen[low][0], *results[-2:]]
        if low == near - 1 and near > 1:
            risen[low - 1], down_sends = tie(risen[low - 1], down_sends)
    down_parts = line_sends(down_sends)
    slopes += part
    outs = jnp.stack(outs, axis=1)

    block = shape((depth, 2, mine, slab, hidden), BF)
    ours, theirs = run(
        functools.partial(weight_kernel, near),
        "weight",
        (block, block),
        [SMEM] + [VMEM] * (3 * near),
        (place, *kept),
        COST["weight"],
        grad_scratch,
    )
    ours, theirs, slopes, down_parts = tie(ours, theirs, slopes, down_parts)
    theirs = swap(theirs, "core", 1)

    resid_slope, mix_slope, out_part = run(
        back_kernel,
        "back",
        (
            shape((span, width), F32),
            shape((seqs, span, width // seqs), BF),
            shape((width, width + LANES), BF),
        ),
        [VMEM] * (8 + len(slopes)),
        (cotangent[0], residual, ffn_in, gates, router_full, small, out_full, mix_low, *slopes),
        COST["back"],
    )
    mix_slope, theirs = tie(mix_slope, theirs)
    mix_slope = lax.all_to_all(mix_slope, SEQ, 0, 0, tiled=True).reshape(length, query_cols)
    sends = joined(ours, theirs)
    mix_slope, sends = tie(mix_slope, sends)
    out_part = lax.psum_scatter(out_part, "row", scatter_dimension=0, tiled=True)
    parts = [line_sends(sends[0])]

    results = run(
        functools.partial(attend_back_kernel, heads, key_heads, scale),
        "attend_back",
        (
            shape((seqs, span, cols), BF),
            *(shape((width // rows, cols + LANES), BF) for _ in range(rows)),
        ),
        [SMEM] + [VMEM] * 7,
        (place, mix_slope, probs, rotated, mix_full, turns, attn_in, proj),
        COST["attend_back"],
        [
            pltpu.VMEM((length, cols), BF),
            pltpu.VMEM((key_heads, HEAD_DIM, length), F32),
            pltpu.VMEM((key_heads, HEAD_DIM, length), F32),
            pltpu.VMEM((width, cols + LANES), BF),
        ],
    )
    results, parts, out_part = tie(results, parts, out_part)
    out_part = lax.psum_scatter(out_part, SEQ, scatter_dimension=0, tiled=True).astype(F32)
    lows_send = results[0]
    row_parts = back_by_rows(results[1:])
    lows = lax.all_to_all(lows_send, SEQ, 0, 0, tiled=True)
    lows, row_parts = tie(lows, row_parts)
    sends[1], outs = after((sends[1], outs), lows)
    more = line_sends(sends[1])
    outs = back_by_rows([outs[mask] for mask in range(rows)])
    outs = run(
        add_kernel,
        "add",
        shape((near, span, width), BF),
        [VMEM] * rows,
        tuple(outs),
        COST["add"],
    )
    outs = [swap(outs[low], "zl", low) if low else outs[0] for low in range(near)]
    parts = [*parts[0], *more, *down_parts]
    part = run(
        add_kernel,
        "add",
        shape((width // rows, cols + LANES), BF),
        [VMEM] * rows,
        tuple(row_parts),
        COST["add"],
    )
    hidden_grad = run(
        last_kernel,
        "last",
        shape((span, width), BF),
        [SMEM] + [VMEM] * 6,
        (place, lows, *wide_halves, small, own, resid_slope),
        COST["last"],
        [pltpu.VMEM((width, seqs * cols), BF)],
    )
    back = lax.all_to_all(part.reshape(seqs, feats, cols + LANES), SEQ, 0, 0, tiled=True)
    back = back.astype(F32)
    hidden_out = run(
        sum_kernel,
        "sum",
        shape((span, width), BF),
        [VMEM] * (1 + len(outs)),
        (residual, *outs),
        COST["sum"],
    )
    attn_gain_grad = jnp.sum(back[:, :, cols], axis=0) / attn_gain.astype(F32)
    query_grad = back[:, :, :query_cols].transpose(1, 0, 2).reshape(feats, HEADS * HEAD_DIM)

    def key_grads(share):
        times = seqs * key_heads // KV_HEADS
        share = share.reshape(seqs // times, times, feats, key_cols).sum(axis=1)
        return share.transpose(1, 0, 2).reshape(feats, KV_HEADS * HEAD_DIM)

    key_grad = key_grads(back[:, :, query_cols : query_cols + key_cols])
    value_grad = key_grads(back[:, :, query_cols + key_cols : cols])
    hidden_grad, hidden_out, parts = tie(hidden_grad, hidden_out, parts)
    gate_grad, up_grad, down_grad = run(
        functools.partial(share_kernel, near),
        "share",
        (
            shape((held, slab, hidden), F32),
            shape((held, slab, hidden), F32),
            shape((held, hidden, slab), F32),
        ),
        [SMEM] + [VMEM] * (3 * depth),
        (place, *parts),
        COST["share"],
    )
    return (
        hidden_out[None],
        hidden_grad[None],
        attn_gain_grad,
        query_grad,
        key_grad,
        value_grad,
        out_part[:, :width].T,
        out_part[:, width + experts],
        out_part[:, width : width + experts],
        gate_grad,
        up_grad,
        down_grad,
    )


COST = {
    "attend": 40,
    "norm": 10,
    "rise": 20,
    "down": 20,
    "fall": 40,
    "weight": 40,
    "join": 5,
    "back": 20,
    "attend_back": 40,
    "last": 10,
    "sum": 3,
    "add": 2,
    "stack": 30,
    "share": 4,
}


def solution(mesh):
    rows, seqs = mesh.shape["row"], mesh.shape["seq"]
    depth = seqs // 2
    held = 16 // rows
    near = min(GROUP, held, depth)
    fine = Mesh(mesh.devices.reshape(rows, depth // near, near, 2), ALL)
    token = P("row", SEQ, None)
    flat, dense = P(ALL), P(ALL, None)
    specs_in = (token, P("row", SEQ), token, token, flat, dense, dense, dense, P(None, ALL), flat, dense)
    specs_out = (token, token, flat, dense, dense, dense, P(None, ALL), flat, dense)
    owned = (token, token, P("row", None, SEQ))
    return jax.shard_map(
        shards,
        mesh=fine,
        in_specs=specs_in + owned,
        out_specs=specs_out + owned,
        check_vma=False,
    )
```

```python
import functools

import jax
import jax.numpy as jnp
import numpy as np
from jax import lax
from jax.experimental import pallas as pl
from jax.experimental.pallas import tpu as pltpu
from jax.sharding import Mesh
from jax.sharding import PartitionSpec as P

HEADS = 16
KV_HEADS = 8
HEAD_DIM = 64
HALF = HEAD_DIM // 2

EPS = 1e-06
THETA = 10000.0
NEG = -1e30
GROUP = 2
LANES = 128
TILE = 16
COUNTS = 160
QUERIES = 256
CHUNK = 256
VMEM_BYTES = 24 * 1024 * 1024
LARGE_BYTES = 60 * 1024 * 1024
LARGE = ("pack", "attend_back")

BF = jnp.bfloat16
F32 = jnp.float32

SEQ = ("zh", "zl", "core")
DEPTH = ("zh", "zl")
ALL = ("row", "zh", "zl", "core")
TEAM = ("row", "zl")

SMEM = pl.BlockSpec(memory_space=pltpu.SMEM)
VMEM = pl.BlockSpec(memory_space=pltpu.VMEM)
ANY = pl.BlockSpec(memory_space=pl.ANY)


def nt(left, right):
    return lax.dot_general(left, right, (((1,), (1,)), ((), ())), preferred_element_type=F32)


def nn(left, right):
    return lax.dot_general(left, right, (((1,), (0,)), ((), ())), preferred_element_type=F32)


def tn(left, right):
    return lax.dot_general(left, right, (((0,), (0,)), ((), ())), preferred_element_type=F32)


def shape(dims, kind):
    return jax.ShapeDtypeStruct(dims, kind)


def run(kernel, name, out_shape, in_specs, args, micros, scratch=()):
    return pl.pallas_call(
        kernel,
        out_shape=out_shape,
        in_specs=in_specs,
        out_specs=jax.tree.map(lambda _: VMEM, out_shape),
        scratch_shapes=list(scratch),
        compiler_params=pltpu.CompilerParams(
            vmem_limit_bytes=LARGE_BYTES if name in LARGE else VMEM_BYTES
        ),
        cost_estimate=pl.CostEstimate(
            flops=int(micros * 1e9), bytes_accessed=1024, transcendentals=0
        ),
        name=name,
    )(*args)


def after(value, *earlier):
    return lax.optimization_barrier((value, *earlier))[0]


def tie(*values):
    return lax.optimization_barrier(values)


def swap(block, axes, mask):
    return lax.ppermute(block, axes, [(i, i ^ mask) for i in range(lax.axis_size(axes))])


def masked(block, axes):
    return [swap(block, axes, mask) if mask else block for mask in range(lax.axis_size(axes))]


def pack_kernel(seqs, query_cols, key_cols, starts, place, query, key, value, router, gain_one, gain_two, segs, out, wide):
    feats = query.shape[0]
    room = out.shape[1] - TILE
    cols = out.shape[2]
    mine = place[3]
    row = lax.broadcasted_iota(jnp.int32, (TILE, LANES), 0)
    lane = lax.broadcasted_iota(jnp.int32, (TILE, LANES), 1)
    times = LANES // feats
    one = jnp.concatenate([gain_one[...].astype(F32)] * times, axis=1)
    two = jnp.concatenate([gain_two[...].astype(F32)] * times, axis=1)
    slot = (row % 8) * times + lane // feats
    gains = jnp.where(slot == mine, jnp.where(row < 8, one, two), 0.0)
    ids = segs[...]
    below_one = jnp.sum((ids < 1).astype(F32), axis=1, keepdims=True)
    below_two = jnp.sum((ids < 2).astype(F32), axis=1, keepdims=True)
    side = lax.broadcasted_iota(jnp.int32, (TILE, HALF), 0)
    counts = jnp.where(side == 0, below_one, jnp.where(side == 1, below_two, 0.0))
    small = [gains, router[...].astype(F32)]
    if feats < HALF:
        small.append(jnp.zeros((TILE, HALF - feats), F32))
    small.append(counts)
    if cols > COUNTS + HALF:
        small.append(jnp.zeros((TILE, cols - COUNTS - HALF), F32))
    small = jnp.concatenate(small, axis=1).astype(BF)
    for number in range(seqs):
        first = starts[number]
        block = jnp.concatenate(
            [
                query[:, number * query_cols : (number + 1) * query_cols].astype(F32),
                key[:, first : first + key_cols].astype(F32),
                value[:, first : first + key_cols].astype(F32),
            ],
            axis=1,
        )
        wide[:, number * cols : (number + 1) * cols] = block.astype(BF)
        if room > feats:
            block = jnp.concatenate([block, jnp.zeros((room - feats, cols), F32)], axis=0)
        out[number, :room] = block.astype(BF)
        out[number, room:] = small


def full_gain(small, first):
    total = jnp.sum(small[:, first : first + 8, :LANES].astype(F32), axis=0)
    return jnp.concatenate([total[i : i + 1] for i in range(8)], axis=1)


def attend_kernel(heads, key_heads, scale, place, freq, proj, small, *refs):
    parts = refs[:-6]
    attn_in, rotated, turns, probs, mix_full, mix_send = refs[-6:]
    span = parts[0].shape[0]
    length = attn_in.shape[0]
    seqs = len(parts)
    gain = full_gain(small[...], 0)
    for number, part in enumerate(parts):
        mask, core = number // 2, number % 2
        spot = (place[1] ^ mask) * 2 + (place[2] ^ core)
        block = part[...].astype(F32)
        inverse = lax.rsqrt(jnp.mean(block * block, axis=-1, keepdims=True) + EPS)
        attn_in[pl.ds(pl.multiple_of(spot * span, span), span), :] = (block * inverse * gain).astype(BF)
    counts = jnp.sum(small[pl.ds(place[0] * seqs, seqs)].astype(F32), axis=0)
    below_one = counts[0:1, COUNTS : COUNTS + 1].astype(jnp.int32)
    below_two = counts[1:2, COUNTS : COUNTS + 1].astype(jnp.int32)
    index = lax.broadcasted_iota(jnp.int32, (length, 1), 0)
    start = jnp.where(index >= below_two, below_two, jnp.where(index >= below_one, below_one, 0))
    angles = (index - start).astype(F32) * freq[...]
    cosine, sine = jnp.cos(angles), jnp.sin(angles)
    turns[...] = jnp.concatenate([cosine, sine], axis=1)
    pre = nn(attn_in[...], proj[...])

    def turned(number):
        first = pre[:, number * HEAD_DIM : number * HEAD_DIM + HALF]
        second = pre[:, number * HEAD_DIM + HALF : (number + 1) * HEAD_DIM]
        return [first * cosine - second * sine, second * cosine + first * sine]

    pieces = []
    for number in range(heads + key_heads):
        pieces += turned(number)
    pieces.append(pre[:, (heads + key_heads) * HEAD_DIM :])
    rotated[...] = jnp.concatenate(pieces, axis=1).astype(BF)
    groups = heads // key_heads
    for number in range(heads):
        kv = number // groups
        key_at = (heads + kv) * HEAD_DIM
        value_at = (heads + key_heads + kv) * HEAD_DIM
        for first in range(0, length, QUERIES):
            rows = slice(first, first + QUERIES)
            keys = first + QUERIES
            query = rotated[rows, number * HEAD_DIM : (number + 1) * HEAD_DIM]
            scores = nt(query, rotated[:keys, key_at : key_at + HEAD_DIM]) * scale
            column = lax.broadcasted_iota(jnp.int32, (QUERIES, keys), 1)
            allowed = (column <= index[rows]) & (column >= start[rows])
            scores = jnp.where(allowed, scores, NEG)
            raised = jnp.exp(scores - jnp.max(scores, axis=-1, keepdims=True))
            weight = (raised / jnp.sum(raised, axis=-1, keepdims=True)).astype(BF)
            probs[number, rows, :keys] = weight
            mix = nn(weight, rotated[:keys, value_at : value_at + HEAD_DIM])
            mix_full[rows, number * HEAD_DIM : (number + 1) * HEAD_DIM] = mix
    for number in range(seqs):
        mix_send[number] = mix_full[number * span : (number + 1) * span].astype(BF)


def put_pieces(place, target, halves):
    for core, half in enumerate(halves):
        for mask in range(half.shape[0]):
            for deep in range(half.shape[1]):
                spot = ((place[0] ^ mask) * half.shape[1] + (place[1] ^ deep)) * 2 + (place[2] ^ core)
                folds = target.shape[1] // half.shape[3]
                feats = half.shape[2] // folds
                rows = pl.ds(pl.multiple_of(spot * feats, feats), feats)
                for fold in range(folds):
                    columns = slice(fold * half.shape[3], (fold + 1) * half.shape[3])
                    target[rows, columns] = half[mask, deep, fold * feats : (fold + 1) * feats]


def norm_kernel(experts, place, mix, own, small, router, routes, half_one, half_two, residual, mix_low, ffn_in, gates, send, out_full):
    span, width = own.shape
    put_pieces(place, out_full, (half_one, half_two))
    mix_low[...] = jnp.concatenate([mix[number] for number in range(mix.shape[0])], axis=1)
    total = own[...].astype(F32) + nt(mix_low[...], out_full[...])
    residual[...] = total
    inverse = lax.rsqrt(jnp.mean(total * total, axis=-1, keepdims=True) + EPS)
    normed = (total * inverse * full_gain(small[...], 8)).astype(BF)
    ffn_in[...] = normed
    logits = nt(normed, router[...])
    number = lax.broadcasted_iota(jnp.int32, (span, experts), 1)
    named = number < 0
    for choice in range(routes.shape[1]):
        named = named | (routes[:, choice : choice + 1] == number)
    logits = jnp.where(named, logits, NEG)
    raised = jnp.where(named, jnp.exp(logits - jnp.max(logits, axis=-1, keepdims=True)), 0.0)
    shares = raised / jnp.sum(raised, axis=-1, keepdims=True)
    gates[...] = shares
    high = shares.astype(BF).astype(F32)
    extra = jnp.concatenate(
        [high, shares - high, jnp.zeros((span, LANES - 2 * experts), F32)], axis=1
    ).astype(BF)
    send[:, :width] = normed
    send[:, width:] = extra


def expert_gate(team, rows, width, experts, expert):
    lane = (lax.broadcasted_iota(jnp.int32, (1, experts), 1) == expert).astype(F32)
    extra = team[rows, width : width + LANES].astype(F32)
    gate = (extra[:, :experts] + extra[:, experts : 2 * experts]) * lane
    return jnp.sum(gate, axis=1, keepdims=True)


def gather_slabs(place, pairs, targets, begin):
    kinds = [(pair, kind) for pair in pairs for kind in range(pair[0].shape[1])]
    for (pair, kind), target in zip(kinds, targets):
        depth, _, _, slab, _ = pair[0].shape
        for core, part in enumerate(pair):
            for mask in range(depth):
                spot = (place[1] ^ mask) * 2 + (place[2] ^ core)
                rows = pl.ds(pl.multiple_of(spot * slab, slab), slab)
                begin(part.at[mask, kind], target.at[:, rows, :])


def copier(sems):
    copies = []

    def begin(source, target):
        copy = pltpu.make_async_copy(source, target, sems.at[len(copies)])
        copy.start()
        copies.append(copy)

    return copies, begin


def rise_kernel(count, low, place, *refs):
    team_parts, up_parts, slabs = refs[:count], refs[count : 2 * count], refs[2 * count : 2 * count + 4]
    team, upstream, act, gate_pres, up_pres, gate_w, up_w, sems = refs[2 * count + 4 :]
    span, width = up_parts[0].shape[1:]
    mine = act.shape[0]
    copies, begin = copier(sems)
    for number in range(count):
        rows = pl.ds(number * span, span)
        begin(team_parts[number], team.at[rows, :])
        begin(up_parts[number].at[low], upstream.at[rows, :])
    gather_slabs(place, (slabs[:2], slabs[2:]), (gate_w, up_w), begin)
    for copy in copies:
        copy.wait()

    def step(number, carry):
        rows = pl.ds(pl.multiple_of(number * CHUNK, CHUNK), CHUNK)
        inputs = team[rows, :width]
        for place_here in range(mine):
            gate_pre = nn(inputs, gate_w[place_here])
            up_pre = nn(inputs, up_w[place_here])
            sigmoid = 1.0 / (1.0 + jnp.exp(-gate_pre))
            act[place_here, rows, :] = (gate_pre * sigmoid * up_pre).astype(BF)
            gate_pres[place_here, rows, :] = gate_pre.astype(BF)
            up_pres[place_here, rows, :] = up_pre.astype(BF)
        return carry

    lax.fori_loop(0, count * span // CHUNK, step, 0)


def fall_kernel(count, held, experts, place, team, upstream, act, gate_pres, up_pres, *refs):
    slabs, slope_parts, out, refs = refs[:6], refs[6 : 6 + count], refs[6 + count], refs[7 + count :]
    gate_low, up_low, slopes, outs, gate_w, up_w, down_w, sems = refs
    tokens, width = upstream.shape
    span = tokens // count
    mine = act.shape[0]
    copies, begin = copier(sems)
    gather_slabs(place, (slabs[:2], slabs[2:4], slabs[4:]), (gate_w, up_w, down_w), begin)
    for copy in copies:
        copy.wait()

    def step(number, carry):
        rows = pl.ds(pl.multiple_of(number * CHUNK, CHUNK), CHUNK)
        up_f = upstream[rows, :].astype(F32)
        out_sum = jnp.zeros((CHUNK, width), F32)
        slope_sum = jnp.zeros((CHUNK, width), F32)
        columns = jnp.zeros((CHUNK, LANES), F32)
        for place_here in range(mine):
            expert = place[0] * held + place[4] * mine + place_here
            gate = expert_gate(team, rows, width, experts, expert)
            expert_out = nt(act[place_here, rows, :], down_w[place_here])
            out_sum = out_sum + gate * expert_out
            score = jnp.sum(up_f * expert_out, axis=1, keepdims=True)
            lane = lax.broadcasted_iota(jnp.int32, (1, LANES), 1)
            columns = jnp.where(lane == expert, score, columns)
            hidden_slope = nn((gate * up_f).astype(BF), down_w[place_here])
            gate_pre = gate_pres[place_here, rows, :].astype(F32)
            up_pre = up_pres[place_here, rows, :].astype(F32)
            sigmoid = 1.0 / (1.0 + jnp.exp(-gate_pre))
            gate_slope = hidden_slope * up_pre * sigmoid * (1.0 + gate_pre * (1.0 - sigmoid))
            gate_slope = gate_slope.astype(BF)
            up_slope = (hidden_slope * gate_pre * sigmoid).astype(BF)
            gate_low[place_here, rows, :] = gate_slope
            up_low[place_here, rows, :] = up_slope
            slope_sum = slope_sum + nt(gate_slope, gate_w[place_here])
            slope_sum = slope_sum + nt(up_slope, up_w[place_here])
        slopes[rows, :width] = slope_sum.astype(BF)
        slopes[rows, width:] = columns.astype(BF)
        outs[rows, :] = out_sum.astype(BF)
        return carry

    lax.fori_loop(0, tokens // CHUNK, step, 0)
    for number in range(count):
        rows = slice(number * span, (number + 1) * span)
        slope_parts[number][...] = slopes[rows, :]
        out[number] = outs[rows, :]


def spread_grad(place, total, kind, number, ours, theirs):
    slab = ours.shape[3]
    for mask in range(ours.shape[0]):
        for core, target in ((0, ours), (1, theirs)):
            spot = (place[1] ^ mask) * 2 + (place[2] ^ core)
            block = total[pl.ds(pl.multiple_of(spot * slab, slab), slab), :]
            target[mask, kind, number] = block.astype(BF)


def down_kernel(halves, held, experts, place, *refs):
    groups = [refs[3 * number : 3 * number + 3] for number in range(halves)]
    ours, theirs, total = refs[3 * halves :]
    mine = groups[0][2].shape[0]
    width = groups[0][1].shape[1]
    for place_here in range(mine):
        expert = place[0] * held + place[4] * mine + place_here
        for number, (team, upstream, act) in enumerate(groups):
            gate = expert_gate(team, slice(None), width, experts, expert)
            grad = tn((gate * upstream[...].astype(F32)).astype(BF), act[place_here])
            if number == 0:
                total[...] = grad
            else:
                total[...] += grad
        spread_grad(place, total, 0, place_here, ours, theirs)


def weight_kernel(halves, place, *refs):
    groups = [refs[3 * number : 3 * number + 3] for number in range(halves)]
    ours, theirs, total = refs[3 * halves :]
    mine = groups[0][1].shape[0]
    width = total.shape[0]
    for kind in range(2):
        for place_here in range(mine):
            for number, (team, *lows) in enumerate(groups):
                grad = tn(team[:, :width], lows[kind][place_here])
                if number == 0:
                    total[...] = grad
                else:
                    total[...] += grad
            spread_grad(place, total, kind, place_here, ours, theirs)


def join_kernel(ours, others, *outs):
    depth = ours.shape[0]
    for number, out in enumerate(outs):
        kind, mask = number // depth, number % depth
        out[...] = (ours[mask, kind].astype(F32) + others[mask, kind].astype(F32)).astype(BF)


def share_kernel(near, place, *refs):
    parts, outs = refs[:-3], refs[-3:]
    depth = len(parts) // 3
    mine = parts[0].shape[0]
    for low in range(near):
        owner = place[4] ^ low
        for number in range(mine):
            for kind, out in enumerate(outs):
                of_kind = parts[kind * depth : (kind + 1) * depth]
                total = sum(part[number].astype(F32) for part in of_kind[low::near])
                out[owner * mine + number] = total if kind < 2 else total.T


def stack_kernel(*refs):
    for number, part in enumerate(refs[:-1]):
        refs[-1][number] = part[...]


def add_kernel(*refs):
    total = refs[0][...].astype(F32)
    for part in refs[1:-1]:
        total = total + part[...].astype(F32)
    refs[-1][...] = total.astype(BF)


def pair_kernel(count, *refs):
    first = 0
    for parts in (refs[:count], refs[count : 2 * count]):
        width = parts[0].shape[1]
        total = sum(part[...].astype(F32) for part in parts)
        refs[-1][:, first : first + width] = total.astype(BF)
        first += width


def sum_kernel(residual, *refs):
    total = residual[...]
    width = total.shape[1]
    for part in refs[:-1]:
        total = total + part[:, part.shape[1] - width :].astype(F32)
    refs[-1][...] = total.astype(BF)


def back_kernel(count, place, cotangent, residual, ffn_in, gates, router, small, out_full, mix_low, *refs):
    slopes, (resid_slope, mix_send) = refs[: -3 - count], refs[-3 - count : -1 - count]
    out_parts, out_part = refs[-1 - count : -1], refs[-1]
    span, width = residual.shape
    experts = gates.shape[1]
    back = slopes[0][:, : width + LANES].astype(F32)
    for part in slopes[1:]:
        back = back + part[:, : width + LANES].astype(F32)
    scores = back[:, width : width + experts]
    shares = gates[...]
    logit_slope = shares * (scores - jnp.sum(shares * scores, axis=-1, keepdims=True))
    logit_slope = logit_slope.astype(BF)
    total = residual[...]
    inverse = lax.rsqrt(jnp.mean(total * total, axis=-1, keepdims=True) + EPS)
    ffn_slope = back[:, :width] + nn(logit_slope, router[...])
    scaled = ffn_slope * full_gain(small[...], 8)
    slope = (
        cotangent[...].astype(F32)
        + inverse * scaled
        - total * (inverse * inverse * inverse) * jnp.mean(scaled * total, axis=-1, keepdims=True)
    )
    resid_slope[...] = slope
    low = slope.astype(BF)
    mix_slope = nn(low, out_full[...]).astype(BF)
    cols = width // mix_send.shape[0]
    for number in range(mix_send.shape[0]):
        mix_send[number] = mix_slope[:, number * cols : (number + 1) * cols]
    out_part[:, :width] = tn(low, mix_low[...]).astype(BF)
    router_part = tn(ffn_in[...], logit_slope)
    gain_part = jnp.sum((ffn_slope * total * inverse).T, axis=1, keepdims=True)
    out_part[:, width:] = jnp.concatenate(
        [router_part, gain_part, jnp.zeros((width, LANES - experts - 1), F32)], axis=1
    ).astype(BF)
    size = width // count
    for mask, part in enumerate(out_parts):
        spot = place[0] ^ mask
        part[...] = out_part[pl.ds(pl.multiple_of(spot * size, size), size), :]


def attend_back_kernel(heads, key_heads, scale, place, slopes, probs, rotated, mix_full, turns, attn_in, proj, lows_send, *refs):
    row_parts, (lows, key_sum, value_sum, part) = refs[:-4], refs[-4:]
    length, width = attn_in.shape
    seqs, span, cols = lows_send.shape
    cosine, sine = turns[:, :HALF], turns[:, HALF:]
    groups = heads // key_heads
    key_sum[...] = jnp.zeros_like(key_sum)
    value_sum[...] = jnp.zeros_like(value_sum)
    for number in range(heads):
        kv = number // groups
        at = slice(number * HEAD_DIM, (number + 1) * HEAD_DIM)
        key_at = (heads + kv) * HEAD_DIM
        value_at = (heads + key_heads + kv) * HEAD_DIM
        for first in range(0, length, QUERIES):
            rows = slice(first, first + QUERIES)
            keys = first + QUERIES
            slope = slopes[rows, at]
            delta = jnp.sum(slope.astype(F32) * mix_full[rows, at], axis=-1, keepdims=True)
            weight = probs[number, rows, :keys]
            weight_slope = nt(slope, rotated[:keys, value_at : value_at + HEAD_DIM])
            low = (weight.astype(F32) * (weight_slope - delta)).astype(BF)
            query = nn(low, rotated[:keys, key_at : key_at + HEAD_DIM]) * scale
            left, right = query[:, :HALF], query[:, HALF:]
            cos_here, sin_here = cosine[rows], sine[rows]
            lows[rows, at] = jnp.concatenate(
                [left * cos_here + right * sin_here, right * cos_here - left * sin_here], axis=1
            ).astype(BF)
            value_sum[kv, :, :keys] += tn(slope, weight)
            key_sum[kv, :, :keys] += tn(rotated[rows, at], low)
    for kv in range(key_heads):
        key = key_sum[kv].T * scale
        left, right = key[:, :HALF], key[:, HALF:]
        at = slice((heads + kv) * HEAD_DIM, (heads + kv + 1) * HEAD_DIM)
        lows[:, at] = jnp.concatenate(
            [left * cosine + right * sine, right * cosine - left * sine], axis=1
        ).astype(BF)
        at = slice((heads + key_heads + kv) * HEAD_DIM, (heads + key_heads + kv + 1) * HEAD_DIM)
        lows[:, at] = value_sum[kv].T.astype(BF)
    for number in range(seqs):
        lows_send[number] = lows[number * span : (number + 1) * span, :]
    grad = tn(attn_in[...], lows[...])
    part[:, :cols] = grad.astype(BF)
    gain_part = jnp.sum(grad * proj[...].astype(F32), axis=1, keepdims=True)
    lane = lax.broadcasted_iota(jnp.int32, (width, LANES), 1)
    part[:, cols:] = jnp.where(lane == 0, gain_part, 0.0).astype(BF)
    size = width // len(row_parts)
    for mask, row_part in enumerate(row_parts):
        spot = place[0] ^ mask
        row_part[...] = part[pl.ds(pl.multiple_of(spot * size, size), size), :]


def last_kernel(place, lows, half_one, half_two, small, own, resid_slope, hidden_grad, wide):
    put_pieces(place, wide, (half_one, half_two))
    joined = jnp.concatenate([lows[number] for number in range(lows.shape[0])], axis=1)
    slope = nt(joined, wide[...])
    block = own[...].astype(F32)
    inverse = lax.rsqrt(jnp.mean(block * block, axis=-1, keepdims=True) + EPS)
    scaled = slope * full_gain(small[...], 0)
    hidden_grad[...] = (
        resid_slope[...]
        + inverse * scaled
        - block * (inverse * inverse * inverse) * jnp.mean(scaled * block, axis=-1, keepdims=True)
    ).astype(BF)


def shards(
    hidden_in,
    segments,
    routes,
    cotangent,
    attn_gain,
    query_weight,
    key_weight,
    value_weight,
    out_weight,
    ffn_gain,
    router_weight,
    gate_weight,
    up_weight,
    down_weight,
):
    rows = lax.axis_size("row")
    far, near, cores = lax.axis_size("zh"), lax.axis_size("zl"), lax.axis_size("core")
    depth = far * near
    seqs = depth * cores
    span, width = hidden_in.shape[1:]
    length = span * seqs
    feats = query_weight.shape[0]
    experts = router_weight.shape[1]
    held, slab, hidden = gate_weight.shape
    mine = held // near
    team_size = rows * near
    tokens = team_size * span
    heads = HEADS // seqs
    groups = HEADS // KV_HEADS
    key_heads = max(1, heads // groups)
    query_cols, key_cols = heads * HEAD_DIM, key_heads * HEAD_DIM
    cols = query_cols + 2 * key_cols
    scale = HEAD_DIM**-0.5
    depth_place = lax.axis_index(DEPTH)
    near_place = lax.axis_index("zl")
    place = jnp.stack(
        [
            lax.axis_index("row"),
            depth_place,
            lax.axis_index("core"),
            lax.axis_index(ALL),
            near_place,
        ]
    ).astype(jnp.int32)
    own = hidden_in[0]

    starts = [(number * heads // groups) * HEAD_DIM for number in range(seqs)]
    room = -(-feats // TILE) * TILE
    packed, wide = run(
        functools.partial(pack_kernel, seqs, query_cols, key_cols, starts),
        "pack",
        (shape((seqs, room + TILE, cols), BF), shape((feats, seqs * cols), BF)),
        [SMEM] + [VMEM] * 7,
        (
            place,
            query_weight,
            key_weight,
            value_weight,
            router_weight.T,
            attn_gain[None],
            ffn_gain[None],
            segments,
        ),
        1,
    )
    line = [own, *(swap(own, DEPTH, mask) for mask in range(1, depth))]
    blocks = []
    for block in line:
        blocks += [block, swap(block, "core", 1)]
    packed = lax.all_to_all(packed, SEQ, 0, 0, tiled=True)
    packed, line[1] = tie(packed, line[1])
    packed = jnp.broadcast_to(packed, (rows, *packed.shape))
    packed = lax.all_to_all(packed, "row", 0, 0).reshape(rows * seqs, room + TILE, cols)
    packed, up_near = tie(packed, masked(cotangent[0], "zl"))
    upstream = masked(jnp.stack(up_near), "row")
    proj = packed[:, :feats].reshape(width, cols)
    small = packed[:, room:]
    router_full = small[:, :, LANES : LANES + feats].transpose(1, 0, 2).reshape(experts, width)


    def row_blocks(block):
        return [block, *(swap(block, "row", mask) for mask in range(1, rows))]

    def near_blocks(block):
        return [block, *(swap(block, "zl", mask) for mask in range(1, near))]


    stacked = jnp.stack([gate_weight, up_weight, down_weight.transpose(0, 2, 1)])
    stacked = stacked.reshape(3, near, mine, slab, hidden)
    stacked = after(stacked, *line)

    def line_slabs(first, last):
        parts = []
        for mask in range(depth):
            part = lax.dynamic_index_in_dim(
                stacked[first:last], near_place ^ (mask % near), 1, False
            )
            parts.append(swap(part, DEPTH, mask) if mask else part)
        return parts

    folded = jnp.concatenate(jnp.split(out_weight.T, width // hidden, axis=1), axis=0)
    size = mine * slab
    gate_line = []
    for mask in range(depth):
        part = lax.dynamic_index_in_dim(stacked[0], near_place ^ (mask % near), 0, False)
        part = jnp.concatenate([part.reshape(size, hidden), folded], axis=0)
        gate_line.append(swap(part, DEPTH, mask) if mask else part)

    freq = THETA ** (-np.arange(HALF, dtype=np.float32) * 2.0 / HEAD_DIM)
    freq = jnp.asarray(freq, F32)[None]
    attn_in, rotated, turns, probs, mix_full, mix_send = run(
        functools.partial(attend_kernel, heads, key_heads, scale),
        "attend",
        (
            shape((length, width), BF),
            shape((length, cols), BF),
            shape((length, HEAD_DIM), F32),
            shape((heads, length, length), BF),
            shape((length, query_cols), F32),
            shape((seqs, span, query_cols), BF),
        ),
        [SMEM] + [VMEM] * (3 + len(blocks)),
        (place, freq, proj, small, *blocks),
        COST["attend"],
    )
    mix_send, gate_line, upstream = tie(mix_send, gate_line, upstream)
    out_line = [part[size:] for part in gate_line]
    gate_line = [part[:size].reshape(1, mine, slab, hidden) for part in gate_line]
    out_rows = masked(jnp.stack(out_line), "row")
    gate_stack = jnp.stack(gate_line)
    gate_other = swap(gate_stack, "core", 1)
    mix = lax.all_to_all(mix_send, SEQ, 0, 0, tiled=True)
    mix, gate_other, out_rows = tie(mix, gate_other, out_rows)
    out_halves = masked(jnp.stack(out_rows), "core")
    up_line = line_slabs(1, 2)

    residual, mix_low, ffn_in, gates, team_send, out_full = run(
        functools.partial(norm_kernel, experts),
        "norm",
        (
            shape((span, width), F32),
            shape((span, width), BF),
            shape((span, width), BF),
            shape((span, experts), F32),
            shape((span, width + LANES), BF),
            shape((width, width), BF),
        ),
        [SMEM] + [VMEM] * 7,
        (place, mix, own, small, router_full, routes[0], *out_halves),
        COST["norm"],
    )
    team = near_blocks(team_send)
    team = [row_blocks(block) for block in team]
    wide_line = masked(wide, DEPTH)
    team[0], wide_line = tie(team[0], wide_line)
    wide_rows = masked(jnp.stack(wide_line), "row")
    up_stack = run(
        stack_kernel,
        "stack",
        shape((depth, 1, mine, slab, hidden), BF),
        [VMEM] * depth,
        tuple(up_line),
        COST["stack"],
    )
    up_other = swap(up_stack, "core", 1)
    down_line = line_slabs(2, 3)

    group_tokens = rows * span
    team_shape, up_shape = shape((group_tokens, width + LANES), BF), shape((group_tokens, width), BF)
    act_shape = shape((mine, group_tokens, hidden), BF)
    weight_scratch = pltpu.VMEM((mine, width, hidden), BF)

    def rise(low):
        return pl.pallas_call(
            functools.partial(rise_kernel, rows, low),
            out_shape=(team_shape, up_shape, act_shape, act_shape, act_shape),
            in_specs=[SMEM] + [ANY] * (2 * rows + 4),
            out_specs=(VMEM,) * 5,
            scratch_shapes=[
                weight_scratch,
                weight_scratch,
                pltpu.SemaphoreType.DMA((2 * rows + 2 * seqs,)),
            ],
            compiler_params=pltpu.CompilerParams(vmem_limit_bytes=VMEM_BYTES),
            cost_estimate=pl.CostEstimate(
                flops=int(COST["rise"] * 1e9), bytes_accessed=1024, transcendentals=0
            ),
            name="rise",
        )(place, *team[low], *upstream, gate_stack, gate_other, up_stack, up_other)

    def fall(risen):
        return pl.pallas_call(
            functools.partial(fall_kernel, rows, held, experts),
            out_shape=(
                *(shape((span, width + LANES), BF) for _ in range(rows)),
                shape((rows, span, width), BF),
                act_shape,
                act_shape,
            ),
            in_specs=[SMEM] + [VMEM] * 5 + [ANY] * 6,
            out_specs=(VMEM,) * (rows + 3),
            scratch_shapes=[
                pltpu.VMEM((group_tokens, width + LANES), BF),
                pltpu.VMEM((group_tokens, width), BF),
                weight_scratch,
                weight_scratch,
                weight_scratch,
                pltpu.SemaphoreType.DMA((3 * seqs,)),
            ],
            compiler_params=pltpu.CompilerParams(vmem_limit_bytes=VMEM_BYTES),
            cost_estimate=pl.CostEstimate(
                flops=int(COST["fall"] * 1e9), bytes_accessed=1024, transcendentals=0
            ),
            name="fall",
        )(place, *risen, gate_stack, gate_other, up_stack, up_other, down_stack, down_other)

    def joined(ours, theirs):
        kinds = ours.shape[1]
        parts = run(
            join_kernel,
            "join",
            tuple(shape((mine, slab, hidden), BF) for _ in range(kinds * depth)),
            [VMEM] * 2,
            (ours, theirs),
            COST["join"],
        )
        return [parts[kind * depth : (kind + 1) * depth] for kind in range(kinds)]

    def line_sends(parts):
        return [swap(part, DEPTH, mask) if mask else part for mask, part in enumerate(parts)]

    risen = []
    for low in range(near):
        results = rise(low)
        if low + 1 < near:
            results, team[low + 1] = tie(results, team[low + 1])
        risen.append(results)
    grad_scratch = [pltpu.VMEM((width, hidden), F32)]
    block = shape((depth, 1, mine, slab, hidden), BF)
    ours, theirs = run(
        functools.partial(down_kernel, near, held, experts),
        "down",
        (block, block),
        [SMEM] + [VMEM] * (3 * near),
        (place, *(value for part in risen for value in part[:3])),
        COST["down"],
        grad_scratch,
    )
    ours, theirs, down_line, wide_rows = tie(ours, theirs, down_line, wide_rows)
    wide_halves = masked(jnp.stack(wide_rows), "core")
    down_stack = jnp.stack(down_line)
    down_other = swap(down_stack, "core", 1)
    theirs = swap(theirs, "core", 1)

    def back_by_rows(group):
        return [swap(part, "row", mask) if mask else part for mask, part in enumerate(group)]

    slopes, outs, kept = [], [None] * near, []
    for low in reversed(range(near)):
        results = fall(risen[low])
        if low == near - 1:
            results, theirs, wide_halves = tie(results, theirs, wide_halves)
            down_sends = joined(ours, theirs)[0]
        else:
            results, part = tie(results, part)
            part = run(
                add_kernel,
                "add",
                shape((span, width + LANES), BF),
                [VMEM] * rows,
                tuple(part),
                COST["add"],
            )
            slopes.append(swap(part, "zl", low + 1))
        part = back_by_rows(results[:rows])
        outs[low] = results[rows]
        kept += [risen[low][0], *results[-2:]]
        if low == near - 1 and near > 1:
            risen[low - 1], down_sends = tie(risen[low - 1], down_sends)
    down_parts = line_sends(down_sends)
    slopes += part
    outs = jnp.stack(outs, axis=1)

    block = shape((depth, 2, mine, slab, hidden), BF)
    ours, theirs = run(
        functools.partial(weight_kernel, near),
        "weight",
        (block, block),
        [SMEM] + [VMEM] * (3 * near),
        (place, *kept),
        COST["weight"],
        grad_scratch,
    )
    ours, theirs, slopes, down_parts = tie(ours, theirs, slopes, down_parts)
    theirs = swap(theirs, "core", 1)

    resid_slope, mix_slope, *out_parts = run(
        functools.partial(back_kernel, rows),
        "back",
        (
            shape((span, width), F32),
            shape((seqs, span, width // seqs), BF),
            *(shape((width // rows, width + LANES), BF) for _ in range(rows)),
        ),
        [SMEM] + [VMEM] * (8 + len(slopes)),
        (place, cotangent[0], residual, ffn_in, gates, router_full, small, out_full, mix_low, *slopes),
        COST["back"],
        [pltpu.VMEM((width, width + LANES), BF)],
    )
    out_parts = back_by_rows(out_parts)
    mix_slope, theirs = tie(mix_slope, theirs)
    mix_slope = lax.all_to_all(mix_slope, SEQ, 0, 0, tiled=True).reshape(length, query_cols)
    sends = joined(ours, theirs)
    mix_slope, sends = tie(mix_slope, sends)
    parts = [line_sends(sends[0])]

    results = run(
        functools.partial(attend_back_kernel, heads, key_heads, scale),
        "attend_back",
        (
            shape((seqs, span, cols), BF),
            *(shape((width // rows, cols + LANES), BF) for _ in range(rows)),
        ),
        [SMEM] + [VMEM] * 7,
        (place, mix_slope, probs, rotated, mix_full, turns, attn_in, proj),
        COST["attend_back"],
        [
            pltpu.VMEM((length, cols), BF),
            pltpu.VMEM((key_heads, HEAD_DIM, length), F32),
            pltpu.VMEM((key_heads, HEAD_DIM, length), F32),
            pltpu.VMEM((width, cols + LANES), BF),
        ],
    )
    results, parts, out_parts = tie(results, parts, out_parts)
    lows_send = results[0]
    row_parts = back_by_rows(results[1:])
    lows = lax.all_to_all(lows_send, SEQ, 0, 0, tiled=True)
    lows, row_parts = tie(lows, row_parts)
    sends[1], outs = after((sends[1], outs), lows)
    more = line_sends(sends[1])
    outs = back_by_rows([outs[mask] for mask in range(rows)])
    outs = run(
        add_kernel,
        "add",
        shape((near, span, width), BF),
        [VMEM] * rows,
        tuple(outs),
        COST["add"],
    )
    outs = [swap(outs[low], "zl", low) if low else outs[0] for low in range(near)]
    parts = [*parts[0], *more, *down_parts]
    part = run(
        functools.partial(pair_kernel, rows),
        "add",
        shape((width // rows, cols + width + 2 * LANES), BF),
        [VMEM] * (2 * rows),
        (*row_parts, *out_parts),
        COST["add"],
    )
    hidden_grad = run(
        last_kernel,
        "last",
        shape((span, width), BF),
        [SMEM] + [VMEM] * 6,
        (place, lows, *wide_halves, small, own, resid_slope),
        COST["last"],
        [pltpu.VMEM((width, seqs * cols), BF)],
    )
    back = lax.all_to_all(part.reshape(seqs, feats, -1), SEQ, 0, 0, tiled=True).astype(F32)
    out_part = jnp.sum(back[:, :, cols + LANES :], axis=0)
    hidden_out = run(
        sum_kernel,
        "sum",
        shape((span, width), BF),
        [VMEM] * (1 + len(outs)),
        (residual, *outs),
        COST["sum"],
    )
    attn_gain_grad = jnp.sum(back[:, :, cols], axis=0) / attn_gain.astype(F32)
    query_grad = back[:, :, :query_cols].transpose(1, 0, 2).reshape(feats, HEADS * HEAD_DIM)

    def key_grads(share):
        times = seqs * key_heads // KV_HEADS
        share = share.reshape(seqs // times, times, feats, key_cols).sum(axis=1)
        return share.transpose(1, 0, 2).reshape(feats, KV_HEADS * HEAD_DIM)

    key_grad = key_grads(back[:, :, query_cols : query_cols + key_cols])
    value_grad = key_grads(back[:, :, query_cols + key_cols : cols])
    hidden_grad, hidden_out, parts = tie(hidden_grad, hidden_out, parts)
    gate_grad, up_grad, down_grad = run(
        functools.partial(share_kernel, near),
        "share",
        (
            shape((held, slab, hidden), F32),
            shape((held, slab, hidden), F32),
            shape((held, hidden, slab), F32),
        ),
        [SMEM] + [VMEM] * (3 * depth),
        (place, *parts),
        COST["share"],
    )
    return (
        hidden_out[None],
        hidden_grad[None],
        attn_gain_grad,
        query_grad,
        key_grad,
        value_grad,
        out_part[:, :width].T,
        out_part[:, width + experts],
        out_part[:, width : width + experts],
        gate_grad,
        up_grad,
        down_grad,
    )


COST = {
    "attend": 40,
    "norm": 10,
    "rise": 20,
    "down": 20,
    "fall": 40,
    "weight": 40,
    "join": 5,
    "back": 20,
    "attend_back": 40,
    "last": 10,
    "sum": 3,
    "add": 2,
    "stack": 30,
    "share": 4,
}


def solution(mesh):
    rows, seqs = mesh.shape["row"], mesh.shape["seq"]
    depth = seqs // 2
    held = 16 // rows
    near = min(GROUP, held, depth)
    fine = Mesh(mesh.devices.reshape(rows, depth // near, near, 2), ALL)
    token = P("row", SEQ, None)
    flat, dense = P(ALL), P(ALL, None)
    specs_in = (token, P("row", SEQ), token, token, flat, dense, dense, dense, P(None, ALL), flat, dense)
    specs_out = (token, token, flat, dense, dense, dense, P(None, ALL), flat, dense)
    owned = (token, token, P("row", None, SEQ))
    return jax.shard_map(
        shards,
        mesh=fine,
        in_specs=specs_in + owned,
        out_specs=specs_out + owned,
        check_vma=False,
    )
```

```python
import functools

import jax
import jax.numpy as jnp
import numpy as np
from jax import lax
from jax.experimental import pallas as pl
from jax.experimental.pallas import tpu as pltpu
from jax.sharding import Mesh
from jax.sharding import PartitionSpec as P

HEADS = 16
KV_HEADS = 8
HEAD_DIM = 64
HALF = HEAD_DIM // 2

EPS = 1e-06
THETA = 10000.0
NEG = -1e30
GROUP = 2
LANES = 128
TILE = 16
COUNTS = 160
QUERIES = 256
CHUNK = 256
VMEM_BYTES = 24 * 1024 * 1024
LARGE_BYTES = 60 * 1024 * 1024
LARGE = ("pack", "attend_back")

BF = jnp.bfloat16
F32 = jnp.float32

SEQ = ("zh", "zl", "core")
DEPTH = ("zh", "zl")
ALL = ("row", "zh", "zl", "core")
TEAM = ("row", "zl")

SMEM = pl.BlockSpec(memory_space=pltpu.SMEM)
VMEM = pl.BlockSpec(memory_space=pltpu.VMEM)
ANY = pl.BlockSpec(memory_space=pl.ANY)


def nt(left, right):
    return lax.dot_general(left, right, (((1,), (1,)), ((), ())), preferred_element_type=F32)


def nn(left, right):
    return lax.dot_general(left, right, (((1,), (0,)), ((), ())), preferred_element_type=F32)


def tn(left, right):
    return lax.dot_general(left, right, (((0,), (0,)), ((), ())), preferred_element_type=F32)


def shape(dims, kind):
    return jax.ShapeDtypeStruct(dims, kind)


def run(kernel, name, out_shape, in_specs, args, micros, scratch=()):
    return pl.pallas_call(
        kernel,
        out_shape=out_shape,
        in_specs=in_specs,
        out_specs=jax.tree.map(lambda _: VMEM, out_shape),
        scratch_shapes=list(scratch),
        compiler_params=pltpu.CompilerParams(
            vmem_limit_bytes=LARGE_BYTES if name in LARGE else VMEM_BYTES
        ),
        cost_estimate=pl.CostEstimate(
            flops=int(micros * 1e9), bytes_accessed=1024, transcendentals=0
        ),
        name=name,
    )(*args)


def after(value, *earlier):
    return lax.optimization_barrier((value, *earlier))[0]


def tie(*values):
    return lax.optimization_barrier(values)


def swap(block, axes, mask):
    return lax.ppermute(block, axes, [(i, i ^ mask) for i in range(lax.axis_size(axes))])


def masked(block, axes):
    return [swap(block, axes, mask) if mask else block for mask in range(lax.axis_size(axes))]


def pack_kernel(seqs, query_cols, key_cols, starts, place, query, key, value, router, gain_one, gain_two, segs, out, wide):
    feats = query.shape[0]
    room = out.shape[1] - TILE
    cols = out.shape[2]
    mine = place[3]
    row = lax.broadcasted_iota(jnp.int32, (TILE, LANES), 0)
    lane = lax.broadcasted_iota(jnp.int32, (TILE, LANES), 1)
    times = LANES // feats
    one = jnp.concatenate([gain_one[...].astype(F32)] * times, axis=1)
    two = jnp.concatenate([gain_two[...].astype(F32)] * times, axis=1)
    slot = (row % 8) * times + lane // feats
    gains = jnp.where(slot == mine, jnp.where(row < 8, one, two), 0.0)
    ids = segs[...]
    below_one = jnp.sum((ids < 1).astype(F32), axis=1, keepdims=True)
    below_two = jnp.sum((ids < 2).astype(F32), axis=1, keepdims=True)
    side = lax.broadcasted_iota(jnp.int32, (TILE, HALF), 0)
    counts = jnp.where(side == 0, below_one, jnp.where(side == 1, below_two, 0.0))
    small = [gains, router[...].astype(F32)]
    if feats < HALF:
        small.append(jnp.zeros((TILE, HALF - feats), F32))
    small.append(counts)
    if cols > COUNTS + HALF:
        small.append(jnp.zeros((TILE, cols - COUNTS - HALF), F32))
    small = jnp.concatenate(small, axis=1).astype(BF)
    for number in range(seqs):
        first = starts[number]
        block = jnp.concatenate(
            [
                query[:, number * query_cols : (number + 1) * query_cols].astype(F32),
                key[:, first : first + key_cols].astype(F32),
                value[:, first : first + key_cols].astype(F32),
            ],
            axis=1,
        )
        wide[:, number * cols : (number + 1) * cols] = block.astype(BF)
        if room > feats:
            block = jnp.concatenate([block, jnp.zeros((room - feats, cols), F32)], axis=0)
        out[number, :room] = block.astype(BF)
        out[number, room:] = small


def full_gain(small, first):
    total = jnp.sum(small[:, first : first + 8, :LANES].astype(F32), axis=0)
    return jnp.concatenate([total[i : i + 1] for i in range(8)], axis=1)


def attend_kernel(heads, key_heads, scale, place, freq, proj, small, *refs):
    parts = refs[:-6]
    attn_in, rotated, turns, probs, mix_full, mix_send = refs[-6:]
    span = parts[0].shape[0]
    length = attn_in.shape[0]
    seqs = len(parts)
    gain = full_gain(small[...], 0)
    for number, part in enumerate(parts):
        mask, core = number // 2, number % 2
        spot = (place[1] ^ mask) * 2 + (place[2] ^ core)
        block = part[...].astype(F32)
        inverse = lax.rsqrt(jnp.mean(block * block, axis=-1, keepdims=True) + EPS)
        attn_in[pl.ds(pl.multiple_of(spot * span, span), span), :] = (block * inverse * gain).astype(BF)
    counts = jnp.sum(small[pl.ds(place[0] * seqs, seqs)].astype(F32), axis=0)
    below_one = counts[0:1, COUNTS : COUNTS + 1].astype(jnp.int32)
    below_two = counts[1:2, COUNTS : COUNTS + 1].astype(jnp.int32)
    index = lax.broadcasted_iota(jnp.int32, (length, 1), 0)
    start = jnp.where(index >= below_two, below_two, jnp.where(index >= below_one, below_one, 0))
    angles = (index - start).astype(F32) * freq[...]
    cosine, sine = jnp.cos(angles), jnp.sin(angles)
    turns[...] = jnp.concatenate([cosine, sine], axis=1)
    pre = nn(attn_in[...], proj[...])

    def turned(number):
        first = pre[:, number * HEAD_DIM : number * HEAD_DIM + HALF]
        second = pre[:, number * HEAD_DIM + HALF : (number + 1) * HEAD_DIM]
        return [first * cosine - second * sine, second * cosine + first * sine]

    pieces = []
    for number in range(heads + key_heads):
        pieces += turned(number)
    pieces.append(pre[:, (heads + key_heads) * HEAD_DIM :])
    rotated[...] = jnp.concatenate(pieces, axis=1).astype(BF)
    groups = heads // key_heads
    for number in range(heads):
        kv = number // groups
        key_at = (heads + kv) * HEAD_DIM
        value_at = (heads + key_heads + kv) * HEAD_DIM
        for first in range(0, length, QUERIES):
            rows = slice(first, first + QUERIES)
            keys = first + QUERIES
            query = rotated[rows, number * HEAD_DIM : (number + 1) * HEAD_DIM]
            scores = nt(query, rotated[:keys, key_at : key_at + HEAD_DIM]) * scale
            column = lax.broadcasted_iota(jnp.int32, (QUERIES, keys), 1)
            allowed = (column <= index[rows]) & (column >= start[rows])
            scores = jnp.where(allowed, scores, NEG)
            raised = jnp.exp(scores - jnp.max(scores, axis=-1, keepdims=True))
            weight = (raised / jnp.sum(raised, axis=-1, keepdims=True)).astype(BF)
            probs[number, rows, :keys] = weight
            mix = nn(weight, rotated[:keys, value_at : value_at + HEAD_DIM])
            mix_full[rows, number * HEAD_DIM : (number + 1) * HEAD_DIM] = mix
    for number in range(seqs):
        mix_send[number] = mix_full[number * span : (number + 1) * span].astype(BF)


def put_pieces(place, target, halves):
    for core, half in enumerate(halves):
        for mask in range(half.shape[0]):
            for deep in range(half.shape[1]):
                spot = ((place[0] ^ mask) * half.shape[1] + (place[1] ^ deep)) * 2 + (place[2] ^ core)
                folds = target.shape[1] // half.shape[3]
                feats = half.shape[2] // folds
                rows = pl.ds(pl.multiple_of(spot * feats, feats), feats)
                for fold in range(folds):
                    columns = slice(fold * half.shape[3], (fold + 1) * half.shape[3])
                    target[rows, columns] = half[mask, deep, fold * feats : (fold + 1) * feats]


def norm_kernel(experts, place, mix, own, small, router, routes, half_one, half_two, residual, mix_low, ffn_in, gates, send, out_full):
    span, width = own.shape
    put_pieces(place, out_full, (half_one, half_two))
    mix_low[...] = jnp.concatenate([mix[number] for number in range(mix.shape[0])], axis=1)
    total = own[...].astype(F32) + nt(mix_low[...], out_full[...])
    residual[...] = total
    inverse = lax.rsqrt(jnp.mean(total * total, axis=-1, keepdims=True) + EPS)
    normed = (total * inverse * full_gain(small[...], 8)).astype(BF)
    ffn_in[...] = normed
    logits = nt(normed, router[...])
    number = lax.broadcasted_iota(jnp.int32, (span, experts), 1)
    named = number < 0
    for choice in range(routes.shape[1]):
        named = named | (routes[:, choice : choice + 1] == number)
    logits = jnp.where(named, logits, NEG)
    raised = jnp.where(named, jnp.exp(logits - jnp.max(logits, axis=-1, keepdims=True)), 0.0)
    shares = raised / jnp.sum(raised, axis=-1, keepdims=True)
    gates[...] = shares
    high = shares.astype(BF).astype(F32)
    extra = jnp.concatenate(
        [high, shares - high, jnp.zeros((span, LANES - 2 * experts), F32)], axis=1
    ).astype(BF)
    send[:, :width] = normed
    send[:, width:] = extra


def expert_gate(team, rows, width, experts, expert):
    lane = (lax.broadcasted_iota(jnp.int32, (1, experts), 1) == expert).astype(F32)
    extra = team[rows, width : width + LANES].astype(F32)
    gate = (extra[:, :experts] + extra[:, experts : 2 * experts]) * lane
    return jnp.sum(gate, axis=1, keepdims=True)


def gather_slabs(place, pairs, targets, begin):
    kinds = [(pair, kind) for pair in pairs for kind in range(pair[0].shape[1])]
    for (pair, kind), target in zip(kinds, targets):
        depth, _, _, slab, _ = pair[0].shape
        for core, part in enumerate(pair):
            for mask in range(depth):
                spot = (place[1] ^ mask) * 2 + (place[2] ^ core)
                rows = pl.ds(pl.multiple_of(spot * slab, slab), slab)
                begin(part.at[mask, kind], target.at[:, rows, :])


def copier(sems):
    copies = []

    def begin(source, target):
        copy = pltpu.make_async_copy(source, target, sems.at[len(copies)])
        copy.start()
        copies.append(copy)

    return copies, begin


def rise_kernel(count, low, place, *refs):
    team_parts, up_parts, slabs = refs[:count], refs[count : 2 * count], refs[2 * count : 2 * count + 4]
    team, upstream, act, gate_pres, up_pres, gate_w, up_w, sems = refs[2 * count + 4 :]
    span, width = up_parts[0].shape[1:]
    mine = act.shape[0]
    copies, begin = copier(sems)
    for number in range(count):
        rows = pl.ds(number * span, span)
        begin(team_parts[number], team.at[rows, :])
        begin(up_parts[number].at[low], upstream.at[rows, :])
    gather_slabs(place, (slabs[:2], slabs[2:]), (gate_w, up_w), begin)
    for copy in copies:
        copy.wait()

    def step(number, carry):
        rows = pl.ds(pl.multiple_of(number * CHUNK, CHUNK), CHUNK)
        inputs = team[rows, :width]
        for place_here in range(mine):
            gate_pre = nn(inputs, gate_w[place_here])
            up_pre = nn(inputs, up_w[place_here])
            sigmoid = 1.0 / (1.0 + jnp.exp(-gate_pre))
            act[place_here, rows, :] = (gate_pre * sigmoid * up_pre).astype(BF)
            gate_pres[place_here, rows, :] = gate_pre.astype(BF)
            up_pres[place_here, rows, :] = up_pre.astype(BF)
        return carry

    lax.fori_loop(0, count * span // CHUNK, step, 0)


def fall_kernel(count, held, experts, place, team, upstream, act, gate_pres, up_pres, *refs):
    slabs, slope_parts, out, refs = refs[:6], refs[6 : 6 + count], refs[6 + count], refs[7 + count :]
    gate_low, up_low, slopes, outs, gate_w, up_w, down_w, sems = refs
    tokens, width = upstream.shape
    span = tokens // count
    mine = act.shape[0]
    copies, begin = copier(sems)
    gather_slabs(place, (slabs[:2], slabs[2:4], slabs[4:]), (gate_w, up_w, down_w), begin)
    for copy in copies:
        copy.wait()

    def step(number, carry):
        rows = pl.ds(pl.multiple_of(number * CHUNK, CHUNK), CHUNK)
        up_f = upstream[rows, :].astype(F32)
        out_sum = jnp.zeros((CHUNK, width), F32)
        slope_sum = jnp.zeros((CHUNK, width), F32)
        columns = jnp.zeros((CHUNK, LANES), F32)
        for place_here in range(mine):
            expert = place[0] * held + place[4] * mine + place_here
            gate = expert_gate(team, rows, width, experts, expert)
            expert_out = nt(act[place_here, rows, :], down_w[place_here])
            out_sum = out_sum + gate * expert_out
            score = jnp.sum(up_f * expert_out, axis=1, keepdims=True)
            lane = lax.broadcasted_iota(jnp.int32, (1, LANES), 1)
            columns = jnp.where(lane == expert, score, columns)
            hidden_slope = nn((gate * up_f).astype(BF), down_w[place_here])
            gate_pre = gate_pres[place_here, rows, :].astype(F32)
            up_pre = up_pres[place_here, rows, :].astype(F32)
            sigmoid = 1.0 / (1.0 + jnp.exp(-gate_pre))
            gate_slope = hidden_slope * up_pre * sigmoid * (1.0 + gate_pre * (1.0 - sigmoid))
            gate_slope = gate_slope.astype(BF)
            up_slope = (hidden_slope * gate_pre * sigmoid).astype(BF)
            gate_low[place_here, rows, :] = gate_slope
            up_low[place_here, rows, :] = up_slope
            slope_sum = slope_sum + nt(gate_slope, gate_w[place_here])
            slope_sum = slope_sum + nt(up_slope, up_w[place_here])
        slopes[rows, :width] = slope_sum.astype(BF)
        slopes[rows, width:] = columns.astype(BF)
        outs[rows, :] = out_sum.astype(BF)
        return carry

    lax.fori_loop(0, tokens // CHUNK, step, 0)
    for number in range(count):
        rows = slice(number * span, (number + 1) * span)
        slope_parts[number][...] = slopes[rows, :]
        out[number] = outs[rows, :]


def spread_grad(place, total, kind, number, ours, theirs):
    slab = ours.shape[3]
    for mask in range(ours.shape[0]):
        for core, target in ((0, ours), (1, theirs)):
            spot = (place[1] ^ mask) * 2 + (place[2] ^ core)
            block = total[pl.ds(pl.multiple_of(spot * slab, slab), slab), :]
            target[mask, kind, number] = block.astype(BF)


def down_kernel(halves, held, experts, place, *refs):
    groups = [refs[3 * number : 3 * number + 3] for number in range(halves)]
    ours, theirs, total = refs[3 * halves :]
    mine = groups[0][2].shape[0]
    width = groups[0][1].shape[1]
    for place_here in range(mine):
        expert = place[0] * held + place[4] * mine + place_here
        for number, (team, upstream, act) in enumerate(groups):
            gate = expert_gate(team, slice(None), width, experts, expert)
            grad = tn((gate * upstream[...].astype(F32)).astype(BF), act[place_here])
            if number == 0:
                total[...] = grad
            else:
                total[...] += grad
        spread_grad(place, total, 0, place_here, ours, theirs)


def weight_kernel(halves, place, *refs):
    groups = [refs[3 * number : 3 * number + 3] for number in range(halves)]
    ours, theirs, total = refs[3 * halves :]
    mine = groups[0][1].shape[0]
    width = total.shape[0]
    for kind in range(2):
        for place_here in range(mine):
            for number, (team, *lows) in enumerate(groups):
                grad = tn(team[:, :width], lows[kind][place_here])
                if number == 0:
                    total[...] = grad
                else:
                    total[...] += grad
            spread_grad(place, total, kind, place_here, ours, theirs)


def join_kernel(ours, others, *outs):
    depth = ours.shape[0]
    for number, out in enumerate(outs):
        kind, mask = number // depth, number % depth
        out[...] = (ours[mask, kind].astype(F32) + others[mask, kind].astype(F32)).astype(BF)


def share_kernel(near, place, *refs):
    parts, outs = refs[:-3], refs[-3:]
    depth = len(parts) // 3
    mine = parts[0].shape[0]
    for low in range(near):
        owner = place[4] ^ low
        for number in range(mine):
            for kind, out in enumerate(outs):
                of_kind = parts[kind * depth : (kind + 1) * depth]
                total = sum(part[number].astype(F32) for part in of_kind[low::near])
                out[owner * mine + number] = total if kind < 2 else total.T


def stack_kernel(*refs):
    for number, part in enumerate(refs[:-1]):
        refs[-1][number] = part[...]


def add_kernel(*refs):
    total = refs[0][...].astype(F32)
    for part in refs[1:-1]:
        total = total + part[...].astype(F32)
    refs[-1][...] = total.astype(BF)


def pair_kernel(count, *refs):
    first = 0
    for parts in (refs[:count], refs[count : 2 * count]):
        width = parts[0].shape[1]
        total = sum(part[...].astype(F32) for part in parts)
        refs[-1][:, first : first + width] = total.astype(BF)
        first += width


def sum_kernel(residual, *refs):
    total = residual[...]
    width = total.shape[1]
    for part in refs[:-1]:
        total = total + part[:, part.shape[1] - width :].astype(F32)
    refs[-1][...] = total.astype(BF)


def back_kernel(count, place, cotangent, residual, ffn_in, gates, router, small, out_full, mix_low, *refs):
    slopes, (resid_slope, mix_send) = refs[: -3 - count], refs[-3 - count : -1 - count]
    out_parts, out_part = refs[-1 - count : -1], refs[-1]
    span, width = residual.shape
    experts = gates.shape[1]
    back = slopes[0][:, : width + LANES].astype(F32)
    for part in slopes[1:]:
        back = back + part[:, : width + LANES].astype(F32)
    scores = back[:, width : width + experts]
    shares = gates[...]
    logit_slope = shares * (scores - jnp.sum(shares * scores, axis=-1, keepdims=True))
    logit_slope = logit_slope.astype(BF)
    total = residual[...]
    inverse = lax.rsqrt(jnp.mean(total * total, axis=-1, keepdims=True) + EPS)
    ffn_slope = back[:, :width] + nn(logit_slope, router[...])
    scaled = ffn_slope * full_gain(small[...], 8)
    slope = (
        cotangent[...].astype(F32)
        + inverse * scaled
        - total * (inverse * inverse * inverse) * jnp.mean(scaled * total, axis=-1, keepdims=True)
    )
    resid_slope[...] = slope
    low = slope.astype(BF)
    mix_slope = nn(low, out_full[...]).astype(BF)
    cols = width // mix_send.shape[0]
    for number in range(mix_send.shape[0]):
        mix_send[number] = mix_slope[:, number * cols : (number + 1) * cols]
    out_part[:, :width] = tn(low, mix_low[...]).astype(BF)
    router_part = tn(ffn_in[...], logit_slope)
    gain_part = jnp.sum((ffn_slope * total * inverse).T, axis=1, keepdims=True)
    out_part[:, width:] = jnp.concatenate(
        [router_part, gain_part, jnp.zeros((width, LANES - experts - 1), F32)], axis=1
    ).astype(BF)
    size = width // count
    for mask, part in enumerate(out_parts):
        spot = place[0] ^ mask
        part[...] = out_part[pl.ds(pl.multiple_of(spot * size, size), size), :]


def attend_back_kernel(heads, key_heads, scale, place, slopes, probs, rotated, mix_full, turns, attn_in, proj, lows_send, *refs):
    row_parts, (lows, key_sum, value_sum, part) = refs[:-4], refs[-4:]
    length, width = attn_in.shape
    seqs, span, cols = lows_send.shape
    cosine, sine = turns[:, :HALF], turns[:, HALF:]
    groups = heads // key_heads
    key_sum[...] = jnp.zeros_like(key_sum)
    value_sum[...] = jnp.zeros_like(value_sum)
    for number in range(heads):
        kv = number // groups
        at = slice(number * HEAD_DIM, (number + 1) * HEAD_DIM)
        key_at = (heads + kv) * HEAD_DIM
        value_at = (heads + key_heads + kv) * HEAD_DIM
        for first in range(0, length, QUERIES):
            rows = slice(first, first + QUERIES)
            keys = first + QUERIES
            slope = slopes[rows, at]
            delta = jnp.sum(slope.astype(F32) * mix_full[rows, at], axis=-1, keepdims=True)
            weight = probs[number, rows, :keys]
            weight_slope = nt(slope, rotated[:keys, value_at : value_at + HEAD_DIM])
            low = (weight.astype(F32) * (weight_slope - delta)).astype(BF)
            query = nn(low, rotated[:keys, key_at : key_at + HEAD_DIM]) * scale
            left, right = query[:, :HALF], query[:, HALF:]
            cos_here, sin_here = cosine[rows], sine[rows]
            lows[rows, at] = jnp.concatenate(
                [left * cos_here + right * sin_here, right * cos_here - left * sin_here], axis=1
            ).astype(BF)
            value_sum[kv, :, :keys] += tn(slope, weight)
            key_sum[kv, :, :keys] += tn(rotated[rows, at], low)
    for kv in range(key_heads):
        key = key_sum[kv].T * scale
        left, right = key[:, :HALF], key[:, HALF:]
        at = slice((heads + kv) * HEAD_DIM, (heads + kv + 1) * HEAD_DIM)
        lows[:, at] = jnp.concatenate(
            [left * cosine + right * sine, right * cosine - left * sine], axis=1
        ).astype(BF)
        at = slice((heads + key_heads + kv) * HEAD_DIM, (heads + key_heads + kv + 1) * HEAD_DIM)
        lows[:, at] = value_sum[kv].T.astype(BF)
    for number in range(seqs):
        lows_send[number] = lows[number * span : (number + 1) * span, :]
    grad = tn(attn_in[...], lows[...])
    part[:, :cols] = grad.astype(BF)
    gain_part = jnp.sum(grad * proj[...].astype(F32), axis=1, keepdims=True)
    lane = lax.broadcasted_iota(jnp.int32, (width, LANES), 1)
    part[:, cols:] = jnp.where(lane == 0, gain_part, 0.0).astype(BF)
    size = width // len(row_parts)
    for mask, row_part in enumerate(row_parts):
        spot = place[0] ^ mask
        row_part[...] = part[pl.ds(pl.multiple_of(spot * size, size), size), :]


def last_kernel(place, lows, half_one, half_two, small, own, resid_slope, hidden_grad, wide):
    put_pieces(place, wide, (half_one, half_two))
    joined = jnp.concatenate([lows[number] for number in range(lows.shape[0])], axis=1)
    slope = nt(joined, wide[...])
    block = own[...].astype(F32)
    inverse = lax.rsqrt(jnp.mean(block * block, axis=-1, keepdims=True) + EPS)
    scaled = slope * full_gain(small[...], 0)
    hidden_grad[...] = (
        resid_slope[...]
        + inverse * scaled
        - block * (inverse * inverse * inverse) * jnp.mean(scaled * block, axis=-1, keepdims=True)
    ).astype(BF)


def shards(
    hidden_in,
    segments,
    routes,
    cotangent,
    attn_gain,
    query_weight,
    key_weight,
    value_weight,
    out_weight,
    ffn_gain,
    router_weight,
    gate_weight,
    up_weight,
    down_weight,
):
    rows = lax.axis_size("row")
    far, near, cores = lax.axis_size("zh"), lax.axis_size("zl"), lax.axis_size("core")
    depth = far * near
    seqs = depth * cores
    span, width = hidden_in.shape[1:]
    length = span * seqs
    feats = query_weight.shape[0]
    experts = router_weight.shape[1]
    held, slab, hidden = gate_weight.shape
    mine = held // near
    team_size = rows * near
    tokens = team_size * span
    heads = HEADS // seqs
    groups = HEADS // KV_HEADS
    key_heads = max(1, heads // groups)
    query_cols, key_cols = heads * HEAD_DIM, key_heads * HEAD_DIM
    cols = query_cols + 2 * key_cols
    scale = HEAD_DIM**-0.5
    depth_place = lax.axis_index(DEPTH)
    near_place = lax.axis_index("zl")
    place = jnp.stack(
        [
            lax.axis_index("row"),
            depth_place,
            lax.axis_index("core"),
            lax.axis_index(ALL),
            near_place,
        ]
    ).astype(jnp.int32)
    own = hidden_in[0]

    starts = [(number * heads // groups) * HEAD_DIM for number in range(seqs)]
    room = -(-feats // TILE) * TILE
    packed, wide = run(
        functools.partial(pack_kernel, seqs, query_cols, key_cols, starts),
        "pack",
        (shape((seqs, room + TILE, cols), BF), shape((feats, seqs * cols), BF)),
        [SMEM] + [VMEM] * 7,
        (
            place,
            query_weight,
            key_weight,
            value_weight,
            router_weight.T,
            attn_gain[None],
            ffn_gain[None],
            segments,
        ),
        1,
    )
    line = [own, *(swap(own, DEPTH, mask) for mask in range(1, depth))]
    packed = lax.all_to_all(packed, SEQ, 0, 0, tiled=True)
    packed = jnp.broadcast_to(packed, (rows, *packed.shape))
    packed = lax.all_to_all(packed, "row", 0, 0).reshape(rows * seqs, room + TILE, cols)
    packed, line[1:], up_near = tie(packed, line[1:], masked(cotangent[0], "zl"))
    blocks = []
    for block in line:
        blocks += [block, swap(block, "core", 1)]
    upstream = masked(jnp.stack(up_near), "row")
    proj = packed[:, :feats].reshape(width, cols)
    small = packed[:, room:]
    router_full = small[:, :, LANES : LANES + feats].transpose(1, 0, 2).reshape(experts, width)


    def row_blocks(block):
        return [block, *(swap(block, "row", mask) for mask in range(1, rows))]

    def near_blocks(block):
        return [block, *(swap(block, "zl", mask) for mask in range(1, near))]


    stacked = jnp.stack([gate_weight, up_weight, down_weight.transpose(0, 2, 1)])
    stacked = stacked.reshape(3, near, mine, slab, hidden)
    stacked = after(stacked, *line)

    def line_slabs(first, last):
        parts = []
        for mask in range(depth):
            part = lax.dynamic_index_in_dim(
                stacked[first:last], near_place ^ (mask % near), 1, False
            )
            parts.append(swap(part, DEPTH, mask) if mask else part)
        return parts

    folded = jnp.concatenate(jnp.split(out_weight.T, width // hidden, axis=1), axis=0)
    size = mine * slab
    gate_line = []
    for mask in range(depth):
        part = lax.dynamic_index_in_dim(stacked[0], near_place ^ (mask % near), 0, False)
        part = jnp.concatenate([part.reshape(size, hidden), folded], axis=0)
        gate_line.append(swap(part, DEPTH, mask) if mask else part)

    freq = THETA ** (-np.arange(HALF, dtype=np.float32) * 2.0 / HEAD_DIM)
    freq = jnp.asarray(freq, F32)[None]
    attn_in, rotated, turns, probs, mix_full, mix_send = run(
        functools.partial(attend_kernel, heads, key_heads, scale),
        "attend",
        (
            shape((length, width), BF),
            shape((length, cols), BF),
            shape((length, HEAD_DIM), F32),
            shape((heads, length, length), BF),
            shape((length, query_cols), F32),
            shape((seqs, span, query_cols), BF),
        ),
        [SMEM] + [VMEM] * (3 + len(blocks)),
        (place, freq, proj, small, *blocks),
        COST["attend"],
    )
    mix_send, gate_line, upstream = tie(mix_send, gate_line, upstream)
    out_line = [part[size:] for part in gate_line]
    gate_line = [part[:size].reshape(1, mine, slab, hidden) for part in gate_line]
    out_rows = masked(jnp.stack(out_line), "row")
    gate_stack = jnp.stack(gate_line)
    gate_other = swap(gate_stack, "core", 1)
    mix = lax.all_to_all(mix_send, SEQ, 0, 0, tiled=True)
    mix, gate_other, out_rows = tie(mix, gate_other, out_rows)
    out_halves = masked(jnp.stack(out_rows), "core")
    up_line = line_slabs(1, 2)

    residual, mix_low, ffn_in, gates, team_send, out_full = run(
        functools.partial(norm_kernel, experts),
        "norm",
        (
            shape((span, width), F32),
            shape((span, width), BF),
            shape((span, width), BF),
            shape((span, experts), F32),
            shape((span, width + LANES), BF),
            shape((width, width), BF),
        ),
        [SMEM] + [VMEM] * 7,
        (place, mix, own, small, router_full, routes[0], *out_halves),
        COST["norm"],
    )
    team = near_blocks(team_send)
    team = [row_blocks(block) for block in team]
    wide_line = masked(wide, DEPTH)
    team[0], wide_line = tie(team[0], wide_line)
    wide_rows = masked(jnp.stack(wide_line), "row")
    up_stack = run(
        stack_kernel,
        "stack",
        shape((depth, 1, mine, slab, hidden), BF),
        [VMEM] * depth,
        tuple(up_line),
        COST["stack"],
    )
    up_other = swap(up_stack, "core", 1)
    down_line = line_slabs(2, 3)

    group_tokens = rows * span
    team_shape, up_shape = shape((group_tokens, width + LANES), BF), shape((group_tokens, width), BF)
    act_shape = shape((mine, group_tokens, hidden), BF)
    weight_scratch = pltpu.VMEM((mine, width, hidden), BF)

    def rise(low):
        return pl.pallas_call(
            functools.partial(rise_kernel, rows, low),
            out_shape=(team_shape, up_shape, act_shape, act_shape, act_shape),
            in_specs=[SMEM] + [ANY] * (2 * rows + 4),
            out_specs=(VMEM,) * 5,
            scratch_shapes=[
                weight_scratch,
                weight_scratch,
                pltpu.SemaphoreType.DMA((2 * rows + 2 * seqs,)),
            ],
            compiler_params=pltpu.CompilerParams(vmem_limit_bytes=VMEM_BYTES),
            cost_estimate=pl.CostEstimate(
                flops=int(COST["rise"] * 1e9), bytes_accessed=1024, transcendentals=0
            ),
            name="rise",
        )(place, *team[low], *upstream, gate_stack, gate_other, up_stack, up_other)

    def fall(risen):
        return pl.pallas_call(
            functools.partial(fall_kernel, rows, held, experts),
            out_shape=(
                *(shape((span, width + LANES), BF) for _ in range(rows)),
                shape((rows, span, width), BF),
                act_shape,
                act_shape,
            ),
            in_specs=[SMEM] + [VMEM] * 5 + [ANY] * 6,
            out_specs=(VMEM,) * (rows + 3),
            scratch_shapes=[
                pltpu.VMEM((group_tokens, width + LANES), BF),
                pltpu.VMEM((group_tokens, width), BF),
                weight_scratch,
                weight_scratch,
                weight_scratch,
                pltpu.SemaphoreType.DMA((3 * seqs,)),
            ],
            compiler_params=pltpu.CompilerParams(vmem_limit_bytes=VMEM_BYTES),
            cost_estimate=pl.CostEstimate(
                flops=int(COST["fall"] * 1e9), bytes_accessed=1024, transcendentals=0
            ),
            name="fall",
        )(place, *risen, gate_stack, gate_other, up_stack, up_other, down_stack, down_other)

    def joined(ours, theirs):
        kinds = ours.shape[1]
        parts = run(
            join_kernel,
            "join",
            tuple(shape((mine, slab, hidden), BF) for _ in range(kinds * depth)),
            [VMEM] * 2,
            (ours, theirs),
            COST["join"],
        )
        return [parts[kind * depth : (kind + 1) * depth] for kind in range(kinds)]

    def line_sends(parts):
        return [swap(part, DEPTH, mask) if mask else part for mask, part in enumerate(parts)]

    risen = []
    for low in range(near):
        results = rise(low)
        if low + 1 < near:
            results, team[low + 1] = tie(results, team[low + 1])
        risen.append(results)
    grad_scratch = [pltpu.VMEM((width, hidden), F32)]
    block = shape((depth, 1, mine, slab, hidden), BF)
    ours, theirs = run(
        functools.partial(down_kernel, near, held, experts),
        "down",
        (block, block),
        [SMEM] + [VMEM] * (3 * near),
        (place, *(value for part in risen for value in part[:3])),
        COST["down"],
        grad_scratch,
    )
    ours, theirs, down_line, wide_rows = tie(ours, theirs, down_line, wide_rows)
    wide_halves = masked(jnp.stack(wide_rows), "core")
    down_stack = jnp.stack(down_line)
    down_other = swap(down_stack, "core", 1)
    theirs = swap(theirs, "core", 1)

    def back_by_rows(group):
        return [swap(part, "row", mask) if mask else part for mask, part in enumerate(group)]

    slopes, outs, kept = [], [None] * near, []
    for low in reversed(range(near)):
        results = fall(risen[low])
        if low == near - 1:
            results, theirs, wide_halves = tie(results, theirs, wide_halves)
            down_sends = joined(ours, theirs)[0]
        else:
            results, part = tie(results, part)
            part = run(
                add_kernel,
                "add",
                shape((span, width + LANES), BF),
                [VMEM] * rows,
                tuple(part),
                COST["add"],
            )
            slopes.append(swap(part, "zl", low + 1))
        part = back_by_rows(results[:rows])
        outs[low] = results[rows]
        kept += [risen[low][0], *results[-2:]]
        if low == near - 1 and near > 1:
            risen[low - 1], down_sends = tie(risen[low - 1], down_sends)
    down_parts = line_sends(down_sends)
    slopes += part
    outs = jnp.stack(outs, axis=1)

    block = shape((depth, 2, mine, slab, hidden), BF)
    ours, theirs = run(
        functools.partial(weight_kernel, near),
        "weight",
        (block, block),
        [SMEM] + [VMEM] * (3 * near),
        (place, *kept),
        COST["weight"],
        grad_scratch,
    )
    ours, theirs, slopes, down_parts = tie(ours, theirs, slopes, down_parts)
    theirs = swap(theirs, "core", 1)

    resid_slope, mix_slope, *out_parts = run(
        functools.partial(back_kernel, rows),
        "back",
        (
            shape((span, width), F32),
            shape((seqs, span, width // seqs), BF),
            *(shape((width // rows, width + LANES), BF) for _ in range(rows)),
        ),
        [SMEM] + [VMEM] * (8 + len(slopes)),
        (place, cotangent[0], residual, ffn_in, gates, router_full, small, out_full, mix_low, *slopes),
        COST["back"],
        [pltpu.VMEM((width, width + LANES), BF)],
    )
    out_parts = back_by_rows(out_parts)
    mix_slope, theirs = tie(mix_slope, theirs)
    mix_slope = lax.all_to_all(mix_slope, SEQ, 0, 0, tiled=True).reshape(length, query_cols)
    sends = joined(ours, theirs)
    mix_slope, sends = tie(mix_slope, sends)
    parts = [line_sends(sends[0])]

    results = run(
        functools.partial(attend_back_kernel, heads, key_heads, scale),
        "attend_back",
        (
            shape((seqs, span, cols), BF),
            *(shape((width // rows, cols + LANES), BF) for _ in range(rows)),
        ),
        [SMEM] + [VMEM] * 7,
        (place, mix_slope, probs, rotated, mix_full, turns, attn_in, proj),
        COST["attend_back"],
        [
            pltpu.VMEM((length, cols), BF),
            pltpu.VMEM((key_heads, HEAD_DIM, length), F32),
            pltpu.VMEM((key_heads, HEAD_DIM, length), F32),
            pltpu.VMEM((width, cols + LANES), BF),
        ],
    )
    results, parts, out_parts = tie(results, parts, out_parts)
    lows_send = results[0]
    row_parts = back_by_rows(results[1:])
    lows = lax.all_to_all(lows_send, SEQ, 0, 0, tiled=True)
    lows, row_parts = tie(lows, row_parts)
    sends[1], outs = after((sends[1], outs), lows)
    more = line_sends(sends[1])
    outs = back_by_rows([outs[mask] for mask in range(rows)])
    outs = run(
        add_kernel,
        "add",
        shape((near, span, width), BF),
        [VMEM] * rows,
        tuple(outs),
        COST["add"],
    )
    outs = [swap(outs[low], "zl", low) if low else outs[0] for low in range(near)]
    parts = [*parts[0], *more, *down_parts]
    part = run(
        functools.partial(pair_kernel, rows),
        "add",
        shape((width // rows, cols + width + 2 * LANES), BF),
        [VMEM] * (2 * rows),
        (*row_parts, *out_parts),
        COST["add"],
    )
    hidden_grad = run(
        last_kernel,
        "last",
        shape((span, width), BF),
        [SMEM] + [VMEM] * 6,
        (place, lows, *wide_halves, small, own, resid_slope),
        COST["last"],
        [pltpu.VMEM((width, seqs * cols), BF)],
    )
    back = lax.all_to_all(part.reshape(seqs, feats, -1), SEQ, 0, 0, tiled=True).astype(F32)
    out_part = jnp.sum(back[:, :, cols + LANES :], axis=0)
    hidden_out = run(
        sum_kernel,
        "sum",
        shape((span, width), BF),
        [VMEM] * (1 + len(outs)),
        (residual, *outs),
        COST["sum"],
    )
    attn_gain_grad = jnp.sum(back[:, :, cols], axis=0) / attn_gain.astype(F32)
    query_grad = back[:, :, :query_cols].transpose(1, 0, 2).reshape(feats, HEADS * HEAD_DIM)

    def key_grads(share):
        times = seqs * key_heads // KV_HEADS
        share = share.reshape(seqs // times, times, feats, key_cols).sum(axis=1)
        return share.transpose(1, 0, 2).reshape(feats, KV_HEADS * HEAD_DIM)

    key_grad = key_grads(back[:, :, query_cols : query_cols + key_cols])
    value_grad = key_grads(back[:, :, query_cols + key_cols : cols])
    hidden_grad, parts, query_grad, key_grad, value_grad, attn_gain_grad, out_part = tie(
        hidden_grad, parts, query_grad, key_grad, value_grad, attn_gain_grad, out_part
    )
    gate_grad, up_grad, down_grad = run(
        functools.partial(share_kernel, near),
        "share",
        (
            shape((held, slab, hidden), F32),
            shape((held, slab, hidden), F32),
            shape((held, hidden, slab), F32),
        ),
        [SMEM] + [VMEM] * (3 * depth),
        (place, *parts),
        COST["share"],
    )
    return (
        hidden_out[None],
        hidden_grad[None],
        attn_gain_grad,
        query_grad,
        key_grad,
        value_grad,
        out_part[:, :width].T,
        out_part[:, width + experts],
        out_part[:, width : width + experts],
        gate_grad,
        up_grad,
        down_grad,
    )


COST = {
    "attend": 40,
    "norm": 10,
    "rise": 20,
    "down": 20,
    "fall": 40,
    "weight": 40,
    "join": 5,
    "back": 20,
    "attend_back": 40,
    "last": 10,
    "sum": 3,
    "add": 2,
    "stack": 30,
    "share": 4,
}


def solution(mesh):
    rows, seqs = mesh.shape["row"], mesh.shape["seq"]
    depth = seqs // 2
    held = 16 // rows
    near = min(GROUP, held, depth)
    fine = Mesh(mesh.devices.reshape(rows, depth // near, near, 2), ALL)
    token = P("row", SEQ, None)
    flat, dense = P(ALL), P(ALL, None)
    specs_in = (token, P("row", SEQ), token, token, flat, dense, dense, dense, P(None, ALL), flat, dense)
    specs_out = (token, token, flat, dense, dense, dense, P(None, ALL), flat, dense)
    owned = (token, token, P("row", None, SEQ))
    return jax.shard_map(
        shards,
        mesh=fine,
        in_specs=specs_in + owned,
        out_specs=specs_out + owned,
        check_vma=False,
    )
```
